256 devices in a mesh: slab: 32 (over y, z_hi, x), pencil: 8 (over z_lo, core).
Axes of the slice: x: 4, y: 4, z: 8 (z_hi: 2, z_lo: 4; z = z_hi * 4 + z_lo), core: 2. Of those that a mesh axis runs over, the one named last changes fastest.
Arguments:
- layer_input: float32 [2, 32, 128, 128, 128], P(None, None, 'slab', 'pencil'), may hold values from -6 to 6
- pre_act: float32 [2, 32, 128, 128, 128], P(None, None, 'slab', 'pencil'), may hold values from -6 to 6
- out_grad: float32 [2, 32, 128, 128, 128], P(None, None, 'slab', 'pencil'), may hold values from -18 to 18
- weight_codes: int32 [32, 32, 32, 2048], P('slab', 'pencil'), may hold values from -127 to 127
- scale_codes: int32 [32, 32, 32, 64], P('slab', 'pencil'), may hold values from 0 to 7
- weight_noise: float32 [32, 32, 32, 2048], P('slab', 'pencil'), may hold values from -1.5 to 1.5
- point_weight: float32 [32, 32], replicated, may hold values from -1 to 1
Outputs:
- grad_input: float32 [2, 32, 128, 128, 128], P(None, None, 'slab', 'pencil')
- grad_spectral: float32 [32, 32, 32, 2048], P('slab', 'pencil')
- grad_point: float32 [32, 32], replicated
- grad_bias: float32 [32], replicated
The draws below stay inside these ranges and needn't reach their ends.
All inputs are finite; a program needn't handle non-finite values.
Results may differ from the reference program's by a relative error of at most 0.00011.
Values sent between devices are 32-bit elements; how exact they have to be, the bound alone decides.
No kernel may reach another device: no remote copies, remote signals or barrier semaphores. Data moves between devices by JAX's collectives and lax.ppermute only.
A program may use at most 128 MiB of HBM per device.

```python
import math
import jax
import jax.numpy as jnp
from jax import lax

C = 32
KX = 32
KY = 32
KZ = 32
NZ = 128
BATCH = 2
NX = 128
NY = 128


def draw_out_grad(key, part):
    key = jax.random.fold_in(key, 7)
    first_key = jax.random.fold_in(key, 0)
    x_ramp = jnp.arange(NX).astype(jnp.float32) / NX
    y_ramp = jnp.arange(NY).astype(jnp.float32) / NY
    ramp = 0.5 + x_ramp[:, None, None] + y_ramp[None, :, None]
    full_shape = (BATCH, C, NX, NY, NZ)
    base_values = jax.random.truncated_normal(first_key, -4.0, 4.0, full_shape, jnp.float32)
    return base_values * ramp


def touch_ends(drawn, own_key, low, top_value):
    dims = drawn.shape
    index_at = [jax.random.randint(jax.random.fold_in(own_key, axis), (), 0, dims[axis]) for axis in range(len(dims))]
    drawn = drawn.at[tuple(index_at)].set(low)
    longest = dims.index(max(dims))
    index_at[longest] = (index_at[longest] + 1) % dims[longest]
    return drawn.at[tuple(index_at)].set(top_value)


def steps_of(stream_key, dims, shards, low, high):
    gain, own = 1.0, jax.random.fold_in(stream_key, 6)
    for dim, parts in shards:
        heights = jnp.exp(jax.random.uniform(jax.random.fold_in(own, dim), (parts,), jnp.float32, low / len(shards), high / len(shards)))
        gain = gain * jnp.repeat(heights, dims[dim] // parts).reshape([-1 if axis == dim else 1 for axis in range(len(dims))])
    return gain


def scatter_about(stream_key, shape, width, bound, cuts=(), held_as=jnp.bfloat16):
    result = jax.random.normal(stream_key, shape, jnp.float32) * width
    if len(cuts) > 0:
        result = steps_of(stream_key, shape, cuts, -0.22, 0.18) * result
    return jnp.clip(result, min=-bound, max=bound).astype(held_as)


def setup_inputs(seed: int = 0) -> dict:
    key_list = jax.random.split(jax.random.key(seed), 8)
    return {
        "layer_input": scatter_about(key_list[0], (BATCH, C, NX, NY, NZ), 1.0, 6.0, ((2, 32), (3, 8)), jnp.float32),
        "pre_act": scatter_about(key_list[1], (BATCH, C, NX, NY, NZ), 1.0, 6.0, ((2, 32), (3, 8)), jnp.float32),
        "out_grad": draw_out_grad(jax.random.fold_in(key_list[7], 71), 0),
        "weight_codes": touch_ends(jax.random.randint(key_list[3], (KZ, KX, KY, 2 * C * C), -127, 128), jax.random.fold_in(key_list[3], 1), -127, 127).astype(jnp.int32),
        "scale_codes": touch_ends(jax.random.randint(key_list[4], (KZ, KX, KY, 2 * C), 0, 8), jax.random.fold_in(key_list[4], 1), 0, 7).astype(jnp.int32),
        "weight_noise": scatter_about(key_list[5], (KZ, KX, KY, 2 * C * C), 0.3, 1.5, ((0, 32), (1, 8)), jnp.float32),
        "point_weight": scatter_about(key_list[6], (C, C), C ** -0.5, 1.0, (), jnp.float32),
    }


HIGHEST = lax.Precision.HIGHEST

def gelu_slope(values):
    cdf_part = 0.5 * (1.0 + lax.erf(values * (1.0 / math.sqrt(2.0))))
    return cdf_part + values * jnp.exp(-0.5 * values * values) * (1.0 / math.sqrt(2.0 * math.pi))

def reference(layer_input, pre_act, out_grad, weight_codes, scale_codes, weight_noise, point_weight):
    grad_out = out_grad * gelu_slope(pre_act)
    cell_count = BATCH * NX * NY * NZ
    grad_point = jnp.einsum('bixyz,boxyz->io', layer_input, grad_out, precision=HIGHEST) / cell_count
    grad_bias = lax.optimization_barrier(jnp.sum(grad_out, axis=(0, 2, 3, 4))) / cell_count
    unit_scale = 1.0 / math.sqrt(NX * NY * NZ)
    kx_index = (jnp.arange(KX) - KX // 2) % NX
    ky_index = (jnp.arange(KY) - KY // 2) % NY

    def forward(field_data):
        z_spectrum = jnp.fft.rfft(field_data, axis=2)[:, :, :KZ]
        y_spectrum = jnp.take(jnp.fft.fft(z_spectrum, axis=1), ky_index, axis=1)
        x_spectrum = jnp.take(jnp.fft.fft(y_spectrum, axis=0), kx_index, axis=0)
        return jnp.transpose(x_spectrum, (2, 0, 1)) * unit_scale

    def spectra(field_data):
        mapped = lax.map(forward, field_data.reshape(BATCH * C, NX, NY, NZ))
        return jnp.transpose(mapped.reshape(BATCH, C, KZ, KX, KY), (2, 3, 4, 0, 1))
    u_hat = spectra(layer_input)
    g_hat = spectra(grad_out)
    code_values = weight_codes.astype(jnp.float32).reshape(KZ, KX, KY, 2, C, C)
    step_size = jnp.exp2(-scale_codes.astype(jnp.float32) / 4.0).reshape(KZ, KX, KY, 2, C, 1) / (16.0 * math.sqrt(C))
    weight = code_values * step_size * (1.0 + weight_noise.reshape(KZ, KX, KY, 2, C, C))
    complex_weight = weight[:, :, :, 0] + 1j * weight[:, :, :, 1]
    q_hat = jnp.einsum('zxyio,zxybo->zxybi', jnp.conj(complex_weight), g_hat, precision=HIGHEST)
    cross_terms = jnp.einsum('zxybi,zxybo->zxyio', u_hat, jnp.conj(g_hat), precision=HIGHEST)
    grad_spectral = jnp.stack([jnp.real(cross_terms), -jnp.imag(cross_terms)], axis=3).reshape(KZ, KX, KY, 2 * C * C)

    def inverse(mode_values):
        full_grid = jnp.zeros((NX, NY, NZ), mode_values.dtype)
        full_grid = full_grid.at[kx_index[:, None, None], ky_index[None, :, None], jnp.arange(KZ)[None, None, :]].set(jnp.transpose(mode_values, (1, 2, 0)))
        return jnp.real(jnp.fft.ifftn(full_grid)) * (NX * NY * NZ * unit_scale)
    q_fields = jnp.transpose(q_hat, (3, 4, 0, 1, 2)).reshape(BATCH * C, KZ, KX, KY)
    spatial = lax.map(inverse, q_fields).reshape(BATCH, C, NX, NY, NZ)
    grad_input = jnp.einsum('bcxyz,ic->bixyz', grad_out, point_weight, precision=HIGHEST) + spatial
    return (grad_input, grad_spectral, grad_point, grad_bias)
```

```python
import math

import jax
import jax.numpy as jnp
import numpy as np
from jax import lax
from jax.experimental import pallas as pl
from jax.experimental.pallas import tpu as pltpu
from jax.sharding import Mesh
from jax.sharding import PartitionSpec as P

HIGH = lax.Precision.HIGH
F32 = jnp.float32
BF16 = jnp.bfloat16
CELLS = 4194304.0
UNIT = 1.0 / math.sqrt(128.0 * 128.0 * 128.0)
PLANE = ("yp", "xp")
COLUMN = ("zh", "zl", "co")


def mm(left, right, left_dim=1, right_dim=0, precision=HIGH):
    dims = (((left_dim,), (right_dim,)), ((), ()))
    return lax.dot_general(left, right, dims, precision=precision, preferred_element_type=F32)


def halves(values):
    top = values.astype(BF16)
    return top, (values - top.astype(F32)).astype(BF16)


def mm_exact(values, pattern):
    top, rest = halves(values)
    return mm(top, pattern, precision=None) + mm(rest, pattern, precision=None)


def wave(frequency, position):
    angle = 2.0 * np.pi * ((frequency * position) % 128) / 128.0
    return np.cos(angle), np.sin(angle)


def z_table():
    d, x, r, h, x2, z = np.ogrid[:16, :2, :2, :2, :2, :128]
    c, s = wave(8 * (d // 4) + 4 * h + d % 4, z)
    return np.where(x == x2, np.where(r == 0, c, -s), 0.0).reshape(128, 256).astype(np.float32)


def z_back_table():
    d, x, r, h, x2, z = np.ogrid[:16, :2, :2, :2, :2, :128]
    c, s = wave(8 * (d // 4) + 4 * h + d % 4, z)
    return np.where(x == x2, np.where(r == 0, c, -s) * UNIT, 0.0).reshape(128, 256).astype(np.float32)


def turn(cosine, sine, r_out, r_in):
    return np.where(r_out == r_in, cosine, np.where(r_out == 0, -sine, sine))


def x_table():
    zh, h2, q, r2, d, x, r, h = np.ogrid[:2, :2, :32, :2, :16, :4, :2, :2]
    c, s = wave(q - 16, 32 * (d // 4) + 16 * zh + 4 * (d % 4) + x)
    return np.where(h == h2, turn(c, -s, r2, r), 0.0).reshape(2, 128, 256).astype(np.float32)


def x_back_table():
    zh, d, x, r2, h2, h, q, r = np.ogrid[:2, :16, :4, :2, :2, :2, :32, :2]
    c, s = wave(q - 16, 32 * (d // 4) + 16 * zh + 4 * (d % 4) + x)
    return np.where(h == h2, turn(c, s, r2, r), 0.0).reshape(2, 256, 128).astype(np.float32)


def y_table():
    odd, r2, k, r, zh, pen, j = np.ogrid[:2, :2, :32, :2, :2, :8, :8]
    c, s = wave(k - 16, 16 * pen + 2 * j + odd)
    return (turn(c, -s, r2, r) * UNIT + 0.0 * zh).reshape(128, 256).astype(np.float32)


def y_back_table():
    r2, pen, j, odd, r, k = np.ogrid[:2, :8, :8, :2, :2, :32]
    c, s = wave(k - 16, 16 * pen + 2 * j + odd)
    return turn(c, s, r2, r).reshape(128, 128).astype(np.float32)


def spread_patterns():
    half, b, c, b2, i, o = np.ogrid[:2, :2, :32, :2, :32, :32]
    same = (half == 0) & (b == b2)
    by_in = (same & (c == i) & (o >= 0)).reshape(128, 2048)
    by_out = (same & (c == o) & (i >= 0)).reshape(128, 2048)
    return by_in.astype(np.float32), by_out.astype(np.float32)


def front_kernel(table, layer, pre, out_grad, grad, message):
    layer, pre, out_grad, grad2 = (ref.reshape(1024, 128) for ref in (layer, pre, out_grad, grad))

    def slope(i, carry):
        rows = pl.ds(pl.multiple_of(i * 64, 64), 64)
        v = pre[rows, :]
        cdf = 0.5 * (1.0 + lax.erf(v * (1.0 / math.sqrt(2.0))))
        bump = v * jnp.exp(-0.5 * v * v) * (1.0 / math.sqrt(2.0 * math.pi))
        grad2[rows, :] = out_grad[rows, :] * (cdf + bump)
        return carry

    lax.fori_loop(0, 16, slope, 0)
    for field, values in ((0, layer), (1, grad2)):
        for j in range(4):
            cells = jnp.concatenate(
                [
                    jnp.concatenate(
                        [values[pl.ds(x * 8 + 2 * j + odd, 64, stride=16), :] for odd in range(2)], 0
                    )
                    for x in range(2)
                ],
                1,
            )
            spectrum = mm(table[...], cells, 1, 1)
            message[:, field, 0, 8 * j : 8 * j + 8, :] = spectrum.reshape(16, 8, 128)


def local_kernel(point, layer, grad, base, sums, products, totals):
    layer, grad, base = (ref.reshape(1024, 128) for ref in (layer, grad, base))
    step = pl.program_id(0) * 2 + pl.program_id(1)

    @pl.when(step == 0)
    def _():
        products[...] = jnp.zeros_like(products)
        totals[...] = jnp.zeros_like(totals)

    for cell in range(0, 16, 2):
        u = jnp.concatenate([layer[pl.ds(cell + k, 64, stride=16), :] for k in range(2)], 1)
        g = jnp.concatenate([grad[pl.ds(cell + k, 64, stride=16), :] for k in range(2)], 1)
        products[...] += mm(u, g, 1, 1)
        totals[...] += g[:, :128] + g[:, 128:]
        mixed = mm(point[...], g)
        for k in range(2):
            base[pl.ds(cell + k, 64, stride=16), :] = mixed[:, 128 * k : 128 * k + 128]

    @pl.when(step == 3)
    def _():
        sums[...] = jnp.zeros_like(sums)
        by_pair = products[0:32, 0:32] + products[32:64, 32:64]
        for k in range(4):
            sums[0, :, 32 * k : 32 * k + 32] = by_pair[8 * k : 8 * k + 8, :]
        bias = mm(jnp.ones((8, 128), F32), totals[...], 1, 1, lax.Precision.HIGHEST)
        sums[1, :, 0:32] = bias[:, 0:32] + bias[:, 32:64]


def weight_kernel(spread, codes, scales, noise, weight):
    step = jnp.exp2(scales[...].astype(F32) * -0.25) * (1.0 / (16.0 * math.sqrt(32.0)))
    top, rest = halves(step)
    last = (step - top.astype(F32) - rest.astype(F32)).astype(BF16)
    wide = sum(mm(part, spread[...], precision=None) for part in (last, rest, top))
    weight[...] = codes[...].astype(F32) * wide * (1.0 + noise[...])


def x_kernel(zh, table, arrived, sums, message):
    field, half = pl.program_id(0), pl.program_id(1)

    @pl.when(field + half == 0)
    def _():
        message[:, 16:18] = jnp.broadcast_to(sums[...][None], (16, 2, 8, 128))

    for j in range(4):
        cells = arrived[:, 0, :, 8 * j : 8 * j + 8, :].reshape(256, 128)
        message[:, field * 8 + half * 4 + j] = mm(table[0], cells).reshape(16, 8, 128)


def along_y(table, arrived):
    rows = arrived.reshape(1024, 128)
    real, imag = [], []
    for kx in range(4):
        cells = jnp.concatenate([rows[pl.ds(2 * kx + r, 128, stride=8), :] for r in range(2)], 0)
        modes = mm(table[...], cells)
        modes = modes[:64] + pltpu.roll(modes[64:], 64, 1)
        real.append(modes[:32])
        imag.append(modes[32:])
    return jnp.concatenate(real, 0), jnp.concatenate(imag, 0)


def mode_kernel(table, back_table, by_out, gather, weight, arrived, g_hat, message):
    g_real, g_imag = along_y(table, arrived)
    g_hat[0] = g_real
    g_hat[1] = g_imag
    q_real = jnp.zeros((128, 128), F32)
    q_imag = jnp.zeros((128, 128), F32)
    for part in range(4):
        lanes = slice(512 * part, 512 * part + 512)
        pairs = 512 * (part % 2)
        wide_real = mm_exact(g_real, by_out[:, lanes])
        wide_imag = mm_exact(g_imag, by_out[:, lanes])
        w_real = weight[:, pairs : pairs + 512]
        w_imag = weight[:, 1024 + pairs : 1536 + pairs]
        q_real += mm_exact(w_real * wide_real + w_imag * wide_imag, gather[lanes, :])
        q_imag += mm_exact(w_real * wide_imag - w_imag * wide_real, gather[lanes, :])
    rows = message.reshape(1024, 128)
    for kx in range(4):
        some = slice(32 * kx, 32 * kx + 32)
        modes = jnp.concatenate([q_real[some], q_imag[some]], 0)
        cells = mm(back_table[...], jnp.concatenate([modes, pltpu.roll(modes, 64, 1)], 0))
        for r in range(2):
            for zh in range(2):
                rows[pl.ds(512 * zh + 2 * kx + r, 64, stride=8), :] = cells[64 * r : 64 * r + 64]


def outer_kernel(table, by_in, by_out, arrived, g_hat, result):
    u_real, u_imag = along_y(table, arrived)
    g_real, g_imag = g_hat[0], g_hat[1]
    for pairs in range(0, 1024, 256):
        real = jnp.zeros((128, 256), F32)
        imag = jnp.zeros((128, 256), F32)
        for b in range(2):
            lanes = slice(1024 * b + pairs, 1024 * b + pairs + 256)
            ur, ui = mm_exact(u_real, by_in[:, lanes]), mm_exact(u_imag, by_in[:, lanes])
            gr, gi = mm_exact(g_real, by_out[:, lanes]), mm_exact(g_imag, by_out[:, lanes])
            real += ur * gr + ui * gi
            imag += ur * gi - ui * gr
        result[:, pairs : pairs + 256] = real
        result[:, 1024 + pairs : 1280 + pairs] = imag


def x_back_kernel(zh, table, arrived, sums, message):
    message[:, 16:18] = jnp.broadcast_to(jnp.sum(sums[...], axis=0)[None], (16, 2, 8, 128))
    for j in range(8):
        cells = mm(table[0], arrived[:, j].reshape(128, 128)).reshape(16, 2, 8, 128)
        message[:, j] = cells[:, 0]
        message[:, 8 + j] = cells[:, 1]


def end_kernel(table, arrived, sums, base, result, grad_point, grad_bias):
    base, result = base.reshape(1024, 128), result.reshape(1024, 128)

    @pl.when(pl.program_id(0) + pl.program_id(1) == 0)
    def _():
        total = jnp.sum(sums[...], axis=0) * (1.0 / CELLS)
        for k in range(4):
            grad_point[8 * k : 8 * k + 8, :] = total[0, :, 32 * k : 32 * k + 32]
        grad_bias[...] = total[1, 0:1, 0:32]

    for j in range(4):
        cells = mm(arrived[:, j].reshape(128, 128), table[...], 0, 0)
        for x in range(2):
            for odd in range(2):
                rows = pl.ds(x * 8 + 2 * j + odd, 64, stride=16)
                result[rows, :] = (
                    base[rows, :] + cells[64 * odd : 64 * odd + 64, 128 * x : 128 * x + 128]
                )


def params(steps=0):
    return pltpu.CompilerParams(
        dimension_semantics=("arbitrary",) * steps if steps else None,
        vmem_limit_bytes=48 * 1024 * 1024,
    )


def cost(flops, moved):
    return pl.CostEstimate(flops=flops, bytes_accessed=moved, transcendentals=0)


def whole(*shape):
    return pl.BlockSpec(shape, lambda *_: (0,) * len(shape))


def shaped(*shape):
    return jax.ShapeDtypeStruct(shape, F32)


def exchange(message, axes):
    return lax.all_to_all(message, axes, split_axis=0, concat_axis=0, tiled=True)


def per_device(
    layer_input, pre_act, out_grad, weight_codes, scale_codes, weight_noise, point_weight
):
    layer, pre, slope_in = (v.reshape(64, 4, 16, 128) for v in (layer_input, pre_act, out_grad))
    zh = lax.axis_index("zh").reshape(1)
    mega = 1 << 20
    field = pl.BlockSpec((64, 2, 8, 128), lambda p, h: (0, p, h, 0))
    grad, message = pl.pallas_call(
        front_kernel,
        grid=(2, 2),
        in_specs=[whole(128, 256), field, field, field],
        out_specs=[field, pl.BlockSpec((16, 2, 1, 32, 128), lambda p, h: (0, 0, p, h, 0))],
        out_shape=[shaped(64, 4, 16, 128), shaped(16, 2, 2, 64, 128)],
        compiler_params=params(2),
        cost_estimate=cost(1 << 30, 10 * mega),
        name="front",
    )(z_table(), layer, pre, slope_in)
    arrived = exchange(message, PLANE)

    blocks = np.kron(np.eye(2, dtype=np.float32), np.ones((32, 32), np.float32))
    both = jnp.tile(point_weight, (2, 2)) * blocks
    base, sums = pl.pallas_call(
        local_kernel,
        grid=(2, 2),
        in_specs=[whole(64, 64), field, field],
        out_specs=[field, whole(2, 8, 128)],
        out_shape=[shaped(64, 4, 16, 128), shaped(2, 8, 128)],
        scratch_shapes=[pltpu.VMEM((64, 64), F32), pltpu.VMEM((64, 128), F32)],
        compiler_params=params(2),
        cost_estimate=cost(1 << 30, 6 * mega),
        name="local",
    )(both, layer, grad)

    spread = np.kron(np.eye(64, dtype=np.float32), np.ones((1, 32), np.float32))
    column = pl.BlockSpec((128, 512), lambda i: (0, i))
    codes, _ = lax.optimization_barrier((weight_codes, sums))
    weight = pl.pallas_call(
        weight_kernel,
        grid=(4,),
        in_specs=[pl.BlockSpec((64, 512), lambda i: (0, i)), column, whole(128, 64), column],
        out_specs=column,
        out_shape=shaped(128, 2048),
        compiler_params=params(1),
        cost_estimate=cost(1 << 27, 3 * mega),
        name="weight",
    )(
        jnp.asarray(spread, BF16),
        codes.reshape(128, 2048),
        scale_codes.reshape(128, 64),
        weight_noise.reshape(128, 2048),
    )

    message = pl.pallas_call(
        x_kernel,
        grid_spec=pltpu.PrefetchScalarGridSpec(
            num_scalar_prefetch=1,
            grid=(2, 2),
            in_specs=[
                pl.BlockSpec((1, 128, 256), lambda f, h, zh: (zh[0], 0, 0)),
                pl.BlockSpec((16, 1, 2, 32, 128), lambda f, h, zh: (0, f, 0, h, 0)),
                whole(2, 8, 128),
            ],
            out_specs=whole(16, 18, 8, 128),
        ),
        out_shape=shaped(16, 18, 8, 128),
        compiler_params=params(2),
        cost_estimate=cost(1 << 29, 3 * mega),
        name="x_modes",
    )(zh, x_table(), arrived, sums)
    arrived = exchange(message, COLUMN)

    by_in, by_out = (jnp.asarray(v, BF16) for v in spread_patterns())
    gather = jnp.asarray(spread_patterns()[0].T, BF16)
    y_modes = jnp.asarray(y_table())
    half = (16, 8, 8, 128)
    g_hat, message = pl.pallas_call(
        mode_kernel,
        grid=(1,),
        in_specs=[
            whole(128, 256),
            whole(128, 128),
            whole(128, 2048),
            whole(2048, 128),
            whole(128, 2048),
            pl.BlockSpec(half, lambda i: (0, 1, 0, 0)),
        ],
        out_specs=[whole(2, 128, 128), whole(*half)],
        out_shape=[shaped(2, 128, 128), shaped(*half)],
        compiler_params=params(1),
        cost_estimate=cost(1 << 30, 4 * mega),
        name="modes",
    )(y_modes, y_back_table(), by_out, gather, weight, arrived)
    returned = exchange(message, COLUMN)

    grad_spectral = pl.pallas_call(
        outer_kernel,
        grid=(1,),
        in_specs=[
            whole(128, 256),
            whole(128, 2048),
            whole(128, 2048),
            pl.BlockSpec(half, lambda i: (0, 0, 0, 0)),
            whole(2, 128, 128),
        ],
        out_specs=whole(128, 2048),
        out_shape=shaped(128, 2048),
        compiler_params=params(1),
        cost_estimate=cost(1 << 30, 4 * mega),
        name="outer",
    )(y_modes, by_in, by_out, arrived, g_hat)

    last_tiles = pl.BlockSpec((16, 2, 8, 128), lambda *_: (0, 8, 0, 0))
    message = pl.pallas_call(
        x_back_kernel,
        grid_spec=pltpu.PrefetchScalarGridSpec(
            num_scalar_prefetch=1,
            grid=(1,),
            in_specs=[
                pl.BlockSpec((1, 256, 128), lambda i, zh: (zh[0], 0, 0)),
                whole(*half),
                last_tiles,
            ],
            out_specs=whole(16, 18, 8, 128),
        ),
        out_shape=shaped(16, 18, 8, 128),
        compiler_params=params(1),
        cost_estimate=cost(1 << 29, 2 * mega),
        name="x_cells",
    )(zh, x_back_table(), returned, arrived)
    returned = exchange(message, PLANE)

    grad_input, grad_point, grad_bias = pl.pallas_call(
        end_kernel,
        grid=(2, 2),
        in_specs=[
            whole(128, 256),
            pl.BlockSpec((16, 4, 8, 128), lambda p, h: (0, 2 * p + h, 0, 0)),
            last_tiles,
            field,
        ],
        out_specs=[field, whole(32, 32), whole(1, 32)],
        out_shape=[shaped(64, 4, 16, 128), shaped(32, 32), shaped(1, 32)],
        compiler_params=params(2),
        cost_estimate=cost(1 << 29, 5 * mega),
        name="end",
    )(z_back_table(), returned, returned, base)
    return (
        grad_input.reshape(layer_input.shape),
        grad_spectral.reshape(weight_codes.shape),
        grad_point,
        grad_bias.reshape(32),
    )


def solution(mesh):
    fine = Mesh(mesh.devices.reshape(4, 2, 4, 4, 2), ("yp", "zh", "xp", "zl", "co"))
    slab, pencil = ("yp", "zh", "xp"), ("zl", "co")
    field, modes = P(None, None, slab, pencil, None), P(slab, pencil, None, None)
    return jax.shard_map(
        per_device,
        mesh=fine,
        in_specs=(field, field, field, modes, modes, modes, P()),
        out_specs=(field, modes, P(), P()),
        check_vma=False,
    )
```

```python
import math

import jax
import jax.numpy as jnp
import numpy as np
from jax import lax
from jax.experimental import pallas as pl
from jax.experimental.pallas import tpu as pltpu
from jax.sharding import Mesh
from jax.sharding import PartitionSpec as P

HIGH = lax.Precision.HIGH
F32 = jnp.float32
BF16 = jnp.bfloat16
CELLS = 4194304.0
UNIT = 1.0 / math.sqrt(128.0 * 128.0 * 128.0)
PLANE = ("yp", "xp")
COLUMN = ("zh", "zl", "co")


def mm(left, right, left_dim=1, right_dim=0, precision=HIGH):
    dims = (((left_dim,), (right_dim,)), ((), ()))
    return lax.dot_general(left, right, dims, precision=precision, preferred_element_type=F32)


def halves(values):
    top = values.astype(BF16)
    return top, (values - top.astype(F32)).astype(BF16)


def mm_exact(values, pattern):
    top, rest = halves(values)
    return mm(top, pattern, precision=None) + mm(rest, pattern, precision=None)


def sine(turns):
    angle = ((turns + 64) & 127) - 64
    angle = jnp.where(angle > 32, 64 - angle, jnp.where(angle < -32, -64 - angle, angle))
    x = angle.astype(F32) * (2.0 * math.pi / 128.0)
    square = x * x
    total = jnp.full_like(x, 1.0 / math.factorial(13))
    for power in (11, 9, 7, 5, 3, 1):
        total = total * square + (-1.0) ** (power // 2) / math.factorial(power)
    return total * x


def grid_of(rows, columns):
    shape = (rows, columns)
    return lax.broadcasted_iota(jnp.int32, shape, 0), lax.broadcasted_iota(jnp.int32, shape, 1)


def z_table(scale):
    row, column = grid_of(128, 256)
    kz = 8 * (row >> 5) + ((row >> 3) & 3) + 4 * (row & 1)
    values = sine(kz * (column & 127) + 32 + 32 * ((row >> 1) & 1))
    return jnp.where(((row >> 2) & 1) == (column >> 7), values * scale, 0.0)


def x_table(zh):
    row, column = grid_of(128, 256)
    cell = 32 * (column >> 6) + 16 * zh + ((column >> 2) & 15)
    quarter = 32 - 32 * (((column >> 1) & 1) - (row & 1))
    values = sine((((row >> 1) & 31) - 16) * cell + quarter)
    return jnp.where((row >> 6) == (column & 1), values, 0.0)


def x_back_table(zh):
    row, column = grid_of(256, 128)
    cell = 32 * (row >> 6) + 16 * zh + ((row >> 2) & 15)
    quarter = 32 + 32 * ((column & 1) - ((row >> 1) & 1))
    values = sine((((column >> 1) & 31) - 16) * cell + quarter)
    return jnp.where((row & 1) == (column >> 6), values, 0.0)


def y_table():
    row, column = grid_of(128, 256)
    cell = 2 * (column & 63) + (row >> 6)
    quarter = 32 - 32 * ((column >> 7) - ((row >> 5) & 1))
    return sine(((row & 31) - 16) * cell + quarter) * UNIT


def y_back_table():
    row, column = grid_of(128, 128)
    cell = 2 * (row & 63) + (column >> 6)
    quarter = 32 + 32 * (((column >> 5) & 1) - (row >> 6))
    return sine(((column & 31) - 16) * cell + quarter)


def pattern(keep):
    return jnp.where(keep, 1.0, 0.0).astype(BF16)


def front_kernel(layer, pre, out_grad, grad, message, table):
    @pl.when(pl.program_id(0) + pl.program_id(1) == 0)
    def _():
        table[...] = z_table(1.0)

    layer, pre, out_grad, grad2 = (ref.reshape(1024, 128) for ref in (layer, pre, out_grad, grad))

    def slope(i, carry):
        rows = pl.ds(pl.multiple_of(i * 64, 64), 64)
        v = pre[rows, :]
        cdf = 0.5 * (1.0 + lax.erf(v * (1.0 / math.sqrt(2.0))))
        bump = v * jnp.exp(-0.5 * v * v) * (1.0 / math.sqrt(2.0 * math.pi))
        grad2[rows, :] = out_grad[rows, :] * (cdf + bump)
        return carry

    lax.fori_loop(0, 16, slope, 0)
    for field, values in ((0, layer), (1, grad2)):
        for j in range(0, 4, 2):
            cells = jnp.concatenate(
                [
                    jnp.concatenate(
                        [values[pl.ds(x * 8 + 2 * j + y, 64, stride=16), :] for y in range(4)], 0
                    )
                    for x in range(2)
                ],
                1,
            )
            spectrum = mm(table[...], cells, 1, 1)
            for k in range(2):
                part = spectrum[:, 128 * k : 128 * k + 128].reshape(16, 8, 128)
                message[:, field, 0, 8 * (j + k) : 8 * (j + k) + 8, :] = part


def local_kernel(point, layer, grad, base, sums, products):
    layer, grad, base = (ref.reshape(1024, 128) for ref in (layer, grad, base))
    step = pl.program_id(0) * 2 + pl.program_id(1)

    @pl.when(step == 0)
    def _():
        products[...] = jnp.zeros_like(products)

    for cell in range(0, 16, 2):
        u = jnp.concatenate([layer[pl.ds(cell + k, 64, stride=16), :] for k in range(2)], 1)
        g = jnp.concatenate([grad[pl.ds(cell + k, 64, stride=16), :] for k in range(2)], 1)
        products[...] += mm(u, g, 1, 1)
        mixed = mm(point[...], g)
        for k in range(2):
            base[pl.ds(cell + k, 64, stride=16), :] = mixed[:, 128 * k : 128 * k + 128]

    @pl.when(step == 3)
    def _():
        by_pair = products[0:32, 0:32] + products[32:64, 32:64]
        for k in range(4):
            sums[:, 32 * k : 32 * k + 32] = by_pair[8 * k : 8 * k + 8, :]


def weight_kernel(spread, codes, scales, noise, weight):
    step = jnp.exp2(scales[...].astype(F32) * -0.25) * (1.0 / (16.0 * math.sqrt(32.0)))
    top, rest = halves(step)
    last = (step - top.astype(F32) - rest.astype(F32)).astype(BF16)
    wide = sum(mm(part, spread[...], precision=None) for part in (last, rest, top))
    weight[...] = codes[...].astype(F32) * wide * (1.0 + noise[...])


def x_kernel(place, arrived, sums, message):
    message[:, 16] = jnp.broadcast_to(sums[...][None], (16, 8, 128))
    table = x_table(place[0])
    for field in range(2):
        for j in range(0, 8, 2):
            cells = jnp.concatenate(
                [
                    arrived[:, field, :, 8 * k : 8 * k + 8, :].reshape(256, 128)
                    for k in (j, j + 1)
                ],
                1,
            )
            modes = mm(table, cells)
            for k in range(2):
                part = modes[:, 128 * k : 128 * k + 128].reshape(16, 8, 128)
                message[:, 8 * field + j + k] = part


def along_y(arrived, field):
    rows = arrived.reshape(2176, 128)
    cells = [
        jnp.concatenate(
            [
                rows[pl.ds(136 * peer + 64 * field + 2 * kx + r, 8, stride=8), :]
                for r in range(2)
                for peer in range(16)
            ],
            0,
        )
        for kx in range(4)
    ]
    modes = mm(y_table(), jnp.concatenate(cells, 1))
    modes = [modes[:, 128 * kx : 128 * kx + 128] for kx in range(4)]
    modes = [part[:64] + pltpu.roll(part[64:], 64, 1) for part in modes]
    real, imag = ([part[32 * r : 32 * r + 32] for part in modes] for r in range(2))
    return jnp.concatenate(real, 0), jnp.concatenate(imag, 0)


def mode_kernel(place, weight, arrived, g_hat, message, sums):
    sums[...] = jnp.sum(arrived[:, 16], axis=0)
    g_real, g_imag = along_y(arrived, 1)
    g_hat[0] = g_real
    g_hat[1] = g_imag
    row, column = grid_of(128, 128)
    row_long, column_long = grid_of(1024, 128)
    gather = pattern((row_long >> 5) == column_long)
    q_real = q_imag = None
    for b in range(2):
        wide = pattern(row == (column & 31) + 32 * b)
        wide_real, wide_imag = mm_exact(g_real, wide), mm_exact(g_imag, wide)
        real = imag = 0.0
        for part in range(4):
            lanes = slice(256 * part, 256 * part + 256)
            w_real = weight[:, 256 * part : 256 * part + 256]
            w_imag = weight[:, 1024 + 256 * part : 1280 + 256 * part]
            gr = jnp.concatenate([wide_real, wide_real], 1)
            gi = jnp.concatenate([wide_imag, wide_imag], 1)
            real += mm_exact(w_real * gr + w_imag * gi, gather[lanes])
            imag += mm_exact(w_real * gi - w_imag * gr, gather[lanes])
        if b == 0:
            q_real, q_imag = real, imag
        else:
            q_real, q_imag = q_real + pltpu.roll(real, 32, 1), q_imag + pltpu.roll(imag, 32, 1)
    rows = message.reshape(1024, 128)
    modes = [
        jnp.concatenate([q_real[32 * kx : 32 * kx + 32], q_imag[32 * kx : 32 * kx + 32]], 0)
        for kx in range(4)
    ]
    modes = [jnp.concatenate([part, pltpu.roll(part, 64, 1)], 0) for part in modes]
    cells = mm(y_back_table(), jnp.concatenate(modes, 1))
    for kx in range(4):
        for r in range(2):
            for zh in range(2):
                part = cells[64 * r : 64 * r + 64, 128 * kx : 128 * kx + 128]
                rows[pl.ds(512 * zh + 2 * kx + r, 64, stride=8), :] = part

    @pl.when(place[2] == 1)
    def _():
        bias = g_real[16:17] + pltpu.roll(g_real[16:17], 96, 1)
        rows[pl.ds(1, 16, stride=64), :] = jnp.broadcast_to(bias * (1.0 / (UNIT * CELLS)), (16, 128))


def outer_kernel(arrived, g_hat, result):
    u_real, u_imag = along_y(arrived, 0)
    row, column = grid_of(128, 128)
    u, g = [], []
    for b in range(2):
        wide = pattern(row == (column & 31) + 32 * b)
        u.append([pltpu.roll(v, 96, 1) if b else v for v in (u_real, u_imag)])
        g.append([mm_exact(g_hat[r], wide) for r in range(2)])
    g = [[jnp.concatenate([v, v], 1) for v in pair] for pair in g]
    row, column = grid_of(128, 256)
    for part in range(4):
        wide = pattern(row == (column >> 5) + 8 * part)
        real = imag = 0.0
        for b in range(2):
            ur, ui = (mm_exact(v, wide) for v in u[b])
            gr, gi = g[b]
            real += ur * gr + ui * gi
            imag += ur * gi - ui * gr
        result[:, 256 * part : 256 * part + 256] = real
        result[:, 1024 + 256 * part : 1280 + 256 * part] = imag


def x_back_kernel(place, arrived, sums, message):
    message[:, 16] = jnp.broadcast_to(sums[...][None], (16, 8, 128))
    table = x_back_table(place[0])
    for j in range(0, 8, 2):
        cells = jnp.concatenate([arrived[:, k].reshape(128, 128) for k in (j, j + 1)], 1)
        cells = mm(table, cells)
        for k in range(2):
            part = cells[:, 128 * k : 128 * k + 128].reshape(16, 2, 8, 128)
            message[:, j + k] = part[:, 0]
            message[:, 8 + j + k] = part[:, 1]

    @pl.when(place[1] == 1)
    def _():
        message[:, 0, 2:3] = jnp.broadcast_to(arrived[4, 0, 1:2][None], (16, 1, 128))


def end_kernel(arrived, sums, base, result, grad_point, grad_bias, table):
    base, result = base.reshape(1024, 128), result.reshape(1024, 128)

    @pl.when(pl.program_id(0) + pl.program_id(1) == 0)
    def _():
        table[...] = z_table(UNIT)
        total = jnp.sum(sums[:, 0], axis=0) * (1.0 / CELLS)
        for k in range(4):
            grad_point[8 * k : 8 * k + 8, :] = total[:, 32 * k : 32 * k + 32]
        grad_bias[...] = arrived[0, 0, 2:3, 0:32]

    for j in range(4):
        cells = mm(arrived[:, j].reshape(128, 128), table[...], 0, 0)
        for x in range(2):
            for odd in range(2):
                rows = pl.ds(x * 8 + 2 * j + odd, 64, stride=16)
                result[rows, :] = (
                    base[rows, :] + cells[64 * odd : 64 * odd + 64, 128 * x : 128 * x + 128]
                )


def params(steps=0, mebibytes=20):
    return pltpu.CompilerParams(
        dimension_semantics=("arbitrary",) * steps if steps else None,
        vmem_limit_bytes=mebibytes << 20,
    )


def cost(flops, moved):
    return pl.CostEstimate(flops=flops, bytes_accessed=moved, transcendentals=0)


def whole(*shape):
    return pl.BlockSpec(shape, lambda *_: (0,) * len(shape))


def shaped(*shape):
    return jax.ShapeDtypeStruct(shape, F32)


def exchange(message, axes):
    return lax.all_to_all(message, axes, split_axis=0, concat_axis=0, tiled=True)


def per_device(
    layer_input, pre_act, out_grad, weight_codes, scale_codes, weight_noise, point_weight
):
    layer, pre, slope_in = (v.reshape(64, 4, 16, 128) for v in (layer_input, pre_act, out_grad))
    plane_first = (lax.axis_index("yp") + lax.axis_index("xp") == 0).astype(jnp.int32)
    owner = plane_first * (lax.axis_index(COLUMN) == 4).astype(jnp.int32)
    place = jnp.stack([lax.axis_index("zh"), plane_first, owner]).astype(jnp.int32)
    mega = 1 << 20
    field = pl.BlockSpec((64, 2, 8, 128), lambda p, h: (0, p, h, 0))
    grad, message = pl.pallas_call(
        front_kernel,
        grid=(2, 2),
        in_specs=[field, field, field],
        out_specs=[field, pl.BlockSpec((16, 2, 1, 32, 128), lambda p, h: (0, 0, p, h, 0))],
        out_shape=[shaped(64, 4, 16, 128), shaped(16, 2, 2, 64, 128)],
        scratch_shapes=[pltpu.VMEM((128, 256), F32)],
        compiler_params=params(2, 60),
        cost_estimate=cost(1 << 30, 10 * mega),
        name="front",
    )(layer, pre, slope_in)
    arrived = exchange(message, PLANE)

    blocks = np.kron(np.eye(2, dtype=np.float32), np.ones((32, 32), np.float32))
    both = jnp.tile(point_weight, (2, 2)) * blocks
    base, sums = pl.pallas_call(
        local_kernel,
        grid=(2, 2),
        in_specs=[whole(64, 64), field, field],
        out_specs=[field, whole(8, 128)],
        out_shape=[shaped(64, 4, 16, 128), shaped(8, 128)],
        scratch_shapes=[pltpu.VMEM((64, 64), F32)],
        compiler_params=params(2),
        cost_estimate=cost(1 << 30, 6 * mega),
        name="local",
    )(both, layer, grad)

    spread = np.kron(np.eye(64, dtype=np.float32), np.ones((1, 32), np.float32))
    column = pl.BlockSpec((128, 512), lambda i: (0, i))
    codes, _ = lax.optimization_barrier((weight_codes, sums))
    weight = pl.pallas_call(
        weight_kernel,
        grid=(4,),
        in_specs=[pl.BlockSpec((64, 512), lambda i: (0, i)), column, whole(128, 64), column],
        out_specs=column,
        out_shape=shaped(128, 2048),
        compiler_params=params(1),
        cost_estimate=cost(1 << 27, 3 * mega),
        name="weight",
    )(
        jnp.asarray(spread, BF16),
        codes.reshape(128, 2048),
        scale_codes.reshape(128, 64),
        weight_noise.reshape(128, 2048),
    )

    def placed(in_specs, out_specs):
        return pltpu.PrefetchScalarGridSpec(
            num_scalar_prefetch=1, grid=(1,), in_specs=in_specs, out_specs=out_specs
        )

    message = pl.pallas_call(
        x_kernel,
        grid_spec=placed([whole(16, 2, 2, 64, 128), whole(8, 128)], whole(16, 17, 8, 128)),
        out_shape=shaped(16, 17, 8, 128),
        compiler_params=params(1),
        cost_estimate=cost(1 << 29, 3 * mega),
        name="x_modes",
    )(place, arrived, sums)
    arrived = exchange(message, COLUMN)

    g_hat, message, sums = pl.pallas_call(
        mode_kernel,
        grid_spec=placed(
            [whole(128, 2048), whole(16, 17, 8, 128)],
            [whole(2, 128, 128), whole(16, 8, 8, 128), whole(8, 128)],
        ),
        out_shape=[shaped(2, 128, 128), shaped(16, 8, 8, 128), shaped(8, 128)],
        compiler_params=params(1),
        cost_estimate=cost(1 << 30, 3 * mega),
        name="modes",
    )(place, weight, arrived)
    returned = exchange(message, COLUMN)

    grad_spectral = pl.pallas_call(
        outer_kernel,
        grid=(1,),
        in_specs=[whole(16, 17, 8, 128), whole(2, 128, 128)],
        out_specs=whole(128, 2048),
        out_shape=shaped(128, 2048),
        compiler_params=params(1),
        cost_estimate=cost(1 << 30, 4 * mega),
        name="outer",
    )(arrived, g_hat)

    message = pl.pallas_call(
        x_back_kernel,
        grid_spec=placed([whole(16, 8, 8, 128), whole(8, 128)], whole(16, 17, 8, 128)),
        out_shape=shaped(16, 17, 8, 128),
        compiler_params=params(1),
        cost_estimate=cost(1 << 29, 2 * mega),
        name="x_cells",
    )(place, returned, sums)
    returned = exchange(message, PLANE)

    grad_input, grad_point, grad_bias = pl.pallas_call(
        end_kernel,
        grid=(2, 2),
        in_specs=[
            pl.BlockSpec((16, 4, 8, 128), lambda p, h: (0, 2 * p + h, 0, 0)),
            pl.BlockSpec((16, 1, 8, 128), lambda p, h: (0, 16, 0, 0)),
            field,
        ],
        out_specs=[field, whole(32, 32), whole(1, 32)],
        out_shape=[shaped(64, 4, 16, 128), shaped(32, 32), shaped(1, 32)],
        scratch_shapes=[pltpu.VMEM((128, 256), F32)],
        compiler_params=params(2, 60),
        cost_estimate=cost(1 << 29, 5 * mega),
        name="end",
    )(returned, returned, base)
    return (
        grad_input.reshape(layer_input.shape),
        grad_spectral.reshape(weight_codes.shape),
        grad_point,
        grad_bias.reshape(32),
    )


def solution(mesh):
    fine = Mesh(mesh.devices.reshape(4, 2, 4, 4, 2), ("yp", "zh", "xp", "zl", "co"))
    slab, pencil = ("yp", "zh", "xp"), ("zl", "co")
    field, modes = P(None, None, slab, pencil, None), P(slab, pencil, None, None)
    return jax.shard_map(
        per_device,
        mesh=fine,
        in_specs=(field, field, field, modes, modes, modes, P()),
        out_specs=(field, modes, P(), P()),
        check_vma=False,
    )
```

```python
import math

import jax
import jax.numpy as jnp
import numpy as np
from jax import lax
from jax.experimental import pallas as pl
from jax.experimental.pallas import tpu as pltpu
from jax.sharding import Mesh
from jax.sharding import PartitionSpec as P

HIGH = lax.Precision.HIGH
F32 = jnp.float32
BF16 = jnp.bfloat16
CELLS = 4194304.0
UNIT = 1.0 / math.sqrt(128.0 * 128.0 * 128.0)
PLANE = ("yp", "xp")
COLUMN = ("zh", "zl", "co")


def mm(left, right, left_dim=1, right_dim=0, precision=HIGH):
    dims = (((left_dim,), (right_dim,)), ((), ()))
    return lax.dot_general(left, right, dims, precision=precision, preferred_element_type=F32)


def halves(values):
    top = values.astype(BF16)
    return top, (values - top.astype(F32)).astype(BF16)


def mm_exact(values, pattern):
    top, rest = halves(values)
    return mm(top, pattern, precision=None) + mm(rest, pattern, precision=None)


def sine(turns):
    angle = ((turns + 64) & 127) - 64
    angle = jnp.where(angle > 32, 64 - angle, jnp.where(angle < -32, -64 - angle, angle))
    x = angle.astype(F32) * (2.0 * math.pi / 128.0)
    square = x * x
    total = jnp.full_like(x, 1.0 / math.factorial(13))
    for power in (11, 9, 7, 5, 3, 1):
        total = total * square + (-1.0) ** (power // 2) / math.factorial(power)
    return total * x


def grid_of(rows, columns):
    shape = (rows, columns)
    return lax.broadcasted_iota(jnp.int32, shape, 0), lax.broadcasted_iota(jnp.int32, shape, 1)


def z_table(scale):
    row, column = grid_of(128, 256)
    kz = 8 * (row >> 5) + ((row >> 3) & 3) + 4 * (row & 1)
    values = sine(kz * (column & 127) + 32 + 32 * ((row >> 1) & 1))
    return jnp.where(((row >> 2) & 1) == (column >> 7), values * scale, 0.0)


def x_table(zh):
    row, column = grid_of(128, 256)
    cell = 32 * (column >> 6) + 16 * zh + ((column >> 2) & 15)
    quarter = 32 - 32 * (((column >> 1) & 1) - (row & 1))
    values = sine((((row >> 1) & 31) - 16) * cell + quarter)
    return jnp.where((row >> 6) == (column & 1), values, 0.0)


def x_back_table(zh):
    row, column = grid_of(256, 128)
    cell = 32 * (row >> 6) + 16 * zh + ((row >> 2) & 15)
    quarter = 32 + 32 * ((column & 1) - ((row >> 1) & 1))
    values = sine((((column >> 1) & 31) - 16) * cell + quarter)
    return jnp.where((row & 1) == (column >> 6), values, 0.0)


def y_table(pencil_of):
    row, column = grid_of(128, 256)
    cell = 16 * pencil_of((column >> 3) & 15) + 2 * (column & 7) + (row >> 6)
    quarter = 32 - 32 * ((column >> 7) - ((row >> 5) & 1))
    return sine(((row & 31) - 16) * cell + quarter) * UNIT


def y_back_table():
    row, column = grid_of(128, 128)
    cell = 2 * (row & 63) + (column >> 6)
    quarter = 32 + 32 * (((column >> 5) & 1) - (row >> 6))
    return sine(((column & 31) - 16) * cell + quarter)


def pattern(keep):
    return jnp.where(keep, 1.0, 0.0).astype(BF16)


def make_grad(pre, out_grad, grad):
    def some(i, carry):
        rows = pl.ds(pl.multiple_of(i * 64, 64), 64)
        v = pre[rows, :]
        cdf = 0.5 * (1.0 + lax.erf(v * (1.0 / math.sqrt(2.0))))
        bump = v * jnp.exp(-0.5 * v * v) * (1.0 / math.sqrt(2.0 * math.pi))
        grad[rows, :] = out_grad[rows, :] * (cdf + bump)
        return carry

    lax.fori_loop(0, grad.shape[0] // 64, some, 0)


def front_kernel(layer, pre, out_grad, message, table, grad2):
    @pl.when(pl.program_id(0) + pl.program_id(1) == 0)
    def _():
        table[...] = z_table(1.0)

    layer, pre, out_grad = (ref.reshape(1024, 128) for ref in (layer, pre, out_grad))
    make_grad(pre, out_grad, grad2)
    for field, values in ((0, layer), (1, grad2)):
        for j in range(0, 4, 2):
            cells = jnp.concatenate(
                [
                    jnp.concatenate(
                        [values[pl.ds(x * 8 + 2 * j + y, 64, stride=16), :] for y in range(4)], 0
                    )
                    for x in range(2)
                ],
                1,
            )
            spectrum = mm(table[...], cells, 1, 1)
            for k in range(2):
                part = spectrum[:, 128 * k : 128 * k + 128].reshape(16, 8, 128)
                message[:, field, 0, 8 * (j + k) : 8 * (j + k) + 8, :] = part


def local_kernel(point, layer, pre, out_grad, base, sums, products, grad):
    layer, pre, out_grad, base = (ref.reshape(1024, 128) for ref in (layer, pre, out_grad, base))
    make_grad(pre, out_grad, grad)
    step = pl.program_id(0) * 2 + pl.program_id(1)

    @pl.when(step == 0)
    def _():
        products[...] = jnp.zeros_like(products)

    for cell in range(0, 16, 2):
        u = jnp.concatenate([layer[pl.ds(cell + k, 64, stride=16), :] for k in range(2)], 1)
        g = jnp.concatenate([grad[pl.ds(cell + k, 64, stride=16), :] for k in range(2)], 1)
        products[...] += mm(u, g, 1, 1)
        mixed = mm(point[...], g)
        for k in range(2):
            base[pl.ds(cell + k, 64, stride=16), :] = mixed[:, 128 * k : 128 * k + 128]

    @pl.when(step == 3)
    def _():
        by_pair = products[0:32, 0:32] + products[32:64, 32:64]
        for k in range(4):
            sums[:, 32 * k : 32 * k + 32] = by_pair[8 * k : 8 * k + 8, :]


def weight_kernel(spread, codes, scales, noise, weight):
    step = jnp.exp2(scales[...].astype(F32) * -0.25) * (1.0 / (16.0 * math.sqrt(32.0)))
    top, rest = halves(step)
    last = (step - top.astype(F32) - rest.astype(F32)).astype(BF16)
    wide = sum(mm(part, spread[...], precision=None) for part in (last, rest, top))
    weight[...] = codes[...].astype(F32) * wide * (1.0 + noise[...])


def along_x(table, arrived, j):
    cells = [arrived[:, 0, :, 8 * k : 8 * k + 8, :].reshape(256, 128) for k in (j, j + 1)]
    return mm(table, jnp.concatenate(cells, 1))


def x_kernel(place, arrived, sums, message):
    message[:, 8] = jnp.broadcast_to(sums[...][None], (16, 8, 128))
    table = x_table(place[0])
    for j in range(0, 8, 2):
        modes = along_x(table, arrived, j)
        for k in range(2):
            message[:, j + k] = modes[:, 128 * k : 128 * k + 128].reshape(16, 8, 128)


def x_side_kernel(place, arrived, keep, give, tiles):
    table = x_table(place[0])
    for j in range(0, 8, 2):
        modes = along_x(table, arrived, j)
        for k in range(2):
            tiles[:, j + k] = modes[:, 128 * k : 128 * k + 128].reshape(16, 8, 128)
    for step in range(8):
        peer = 2 * ((place[3] + step) & 7)
        keep[step] = tiles[peer + place[4]]
        give[step] = tiles[peer + 1 - place[4]]


def pair_kernel(keep, got, *pairs):
    for step, pair in enumerate(pairs):
        pair[0] = keep[step]
        pair[1] = got[step]


def along_y(table, pieces):
    cells = [
        jnp.concatenate(
            [rows[pl.ds(at + 2 * kx + r, 8, stride=8), :] for r in range(2) for rows, at in pieces], 0
        )
        for kx in range(4)
    ]
    modes = mm(table, jnp.concatenate(cells, 1))
    modes = [modes[:, 128 * kx : 128 * kx + 128] for kx in range(4)]
    modes = [part[:64] + pltpu.roll(part[64:], 64, 1) for part in modes]
    real, imag = ([part[32 * r : 32 * r + 32] for part in modes] for r in range(2))
    return jnp.concatenate(real, 0), jnp.concatenate(imag, 0)


def mode_kernel(place, weight, arrived, g_hat, message, sums):
    sums[...] = jnp.sum(arrived[:, 8], axis=0)
    sources = arrived.reshape(1152, 128)
    table = y_table(lambda source: source & 7)
    g_real, g_imag = along_y(table, [(sources, 72 * peer) for peer in range(16)])
    g_hat[0] = g_real
    g_hat[1] = g_imag
    row, column = grid_of(128, 128)
    row_long, column_long = grid_of(1024, 128)
    gather = pattern((row_long >> 5) == column_long)
    q_real = q_imag = None
    for b in range(2):
        wide = pattern(row == (column & 31) + 32 * b)
        wide_real, wide_imag = mm_exact(g_real, wide), mm_exact(g_imag, wide)
        real = imag = 0.0
        for part in range(4):
            lanes = slice(256 * part, 256 * part + 256)
            w_real = weight[:, 256 * part : 256 * part + 256]
            w_imag = weight[:, 1024 + 256 * part : 1280 + 256 * part]
            gr = jnp.concatenate([wide_real, wide_real], 1)
            gi = jnp.concatenate([wide_imag, wide_imag], 1)
            real += mm_exact(w_real * gr + w_imag * gi, gather[lanes])
            imag += mm_exact(w_real * gi - w_imag * gr, gather[lanes])
        if b == 0:
            q_real, q_imag = real, imag
        else:
            q_real, q_imag = q_real + pltpu.roll(real, 32, 1), q_imag + pltpu.roll(imag, 32, 1)
    rows = message.reshape(1024, 128)
    modes = [
        jnp.concatenate([q_real[32 * kx : 32 * kx + 32], q_imag[32 * kx : 32 * kx + 32]], 0)
        for kx in range(4)
    ]
    modes = [jnp.concatenate([part, pltpu.roll(part, 64, 1)], 0) for part in modes]
    cells = mm(y_back_table(), jnp.concatenate(modes, 1))
    for kx in range(4):
        for r in range(2):
            for zh in range(2):
                part = cells[64 * r : 64 * r + 64, 128 * kx : 128 * kx + 128]
                rows[pl.ds(512 * zh + 2 * kx + r, 64, stride=8), :] = part

    @pl.when(place[2] == 1)
    def _():
        bias = g_real[16:17] + pltpu.roll(g_real[16:17], 96, 1)
        rows[pl.ds(1, 16, stride=64), :] = jnp.broadcast_to(bias * (1.0 / (UNIT * CELLS)), (16, 128))


def outer_kernel(place, *refs):
    *pairs, g_hat, result = refs

    def pencil(source):
        return 2 * ((place[3] - (source >> 1)) & 3) + ((source & 1) ^ place[4])

    pieces = [(pair.reshape(128, 128), 64 * k) for pair in pairs for k in range(2)]
    u_real, u_imag = along_y(y_table(pencil), pieces)
    row, column = grid_of(128, 128)
    u, g = [], []
    for b in range(2):
        wide = pattern(row == (column & 31) + 32 * b)
        u.append([pltpu.roll(v, 96, 1) if b else v for v in (u_real, u_imag)])
        g.append([mm_exact(g_hat[r], wide) for r in range(2)])
    g = [[jnp.concatenate([v, v], 1) for v in pair] for pair in g]
    row, column = grid_of(128, 256)
    for part in range(4):
        wide = pattern(row == (column >> 5) + 8 * part)
        real = imag = 0.0
        for b in range(2):
            ur, ui = (mm_exact(v, wide) for v in u[b])
            gr, gi = g[b]
            real += ur * gr + ui * gi
            imag += ur * gi - ui * gr
        result[:, 256 * part : 256 * part + 256] = real
        result[:, 1024 + 256 * part : 1280 + 256 * part] = imag


def x_back_kernel(place, arrived, sums, message):
    message[:, 16] = jnp.broadcast_to(sums[...][None], (16, 8, 128))
    table = x_back_table(place[0])
    for j in range(0, 8, 2):
        cells = jnp.concatenate([arrived[:, k].reshape(128, 128) for k in (j, j + 1)], 1)
        cells = mm(table, cells)
        for k in range(2):
            part = cells[:, 128 * k : 128 * k + 128].reshape(16, 2, 8, 128)
            message[:, j + k] = part[:, 0]
            message[:, 8 + j + k] = part[:, 1]

    @pl.when(place[1] == 1)
    def _():
        message[:, 0, 2:3] = jnp.broadcast_to(arrived[4, 0, 1:2][None], (16, 1, 128))


def end_kernel(arrived, sums, base, result, grad_point, grad_bias, table, held, taken):
    result = result.reshape(1024, 128)
    step = 2 * pl.program_id(0) + pl.program_id(1)

    def load(n):
        there = base.at[:, pl.ds(2 * (n // 2), 2), pl.ds(8 * (n % 2), 8), :]
        return pltpu.make_async_copy(there, held.at[n], taken.at[n])

    @pl.when(step == 0)
    def _():
        for n in range(4):
            load(n).start()
        table[...] = z_table(UNIT)
        total = jnp.sum(sums[:, 0], axis=0) * (1.0 / CELLS)
        for k in range(4):
            grad_point[8 * k : 8 * k + 8, :] = total[:, 32 * k : 32 * k + 32]
        grad_bias[...] = arrived[0, 0, 2:3, 0:32]

    for n in range(4):

        @pl.when(step == n)
        def _():
            load(n).wait()
            rest = held.at[n].reshape(1024, 128)
            for j in range(4):
                cells = mm(arrived[:, j].reshape(128, 128), table[...], 0, 0)
                for x in range(2):
                    for odd in range(2):
                        rows = pl.ds(x * 8 + 2 * j + odd, 64, stride=16)
                        part = cells[64 * odd : 64 * odd + 64, 128 * x : 128 * x + 128]
                        result[rows, :] = rest[rows, :] + part


def params(steps=0, mebibytes=20):
    return pltpu.CompilerParams(
        dimension_semantics=("arbitrary",) * steps if steps else None,
        vmem_limit_bytes=mebibytes << 20,
    )


def cost(flops, moved):
    return pl.CostEstimate(flops=flops, bytes_accessed=moved, transcendentals=0)


def whole(*shape):
    return pl.BlockSpec(shape, lambda *_: (0,) * len(shape))


def shaped(*shape):
    return jax.ShapeDtypeStruct(shape, F32)


def exchange(message, axes):
    return lax.all_to_all(message, axes, split_axis=0, concat_axis=0, tiled=True)


def per_device(
    layer_input, pre_act, out_grad, weight_codes, scale_codes, weight_noise, point_weight
):
    layer, pre, slope_in = (v.reshape(64, 4, 16, 128) for v in (layer_input, pre_act, out_grad))
    plane_first = (lax.axis_index("yp") + lax.axis_index("xp") == 0).astype(jnp.int32)
    owner = plane_first * (lax.axis_index(COLUMN) == 4).astype(jnp.int32)
    chip, core = lax.axis_index(("zh", "zl")), lax.axis_index("co")
    place = jnp.stack([lax.axis_index("zh"), plane_first, owner, chip, core]).astype(jnp.int32)
    mega = 1 << 20
    field = pl.BlockSpec((64, 2, 8, 128), lambda p, h: (0, p, h, 0))
    message = pl.pallas_call(
        front_kernel,
        grid=(2, 2),
        in_specs=[field, field, field],
        out_specs=pl.BlockSpec((16, 2, 1, 32, 128), lambda p, h: (0, 0, p, h, 0)),
        out_shape=shaped(16, 2, 2, 64, 128),
        scratch_shapes=[pltpu.VMEM((128, 256), F32), pltpu.VMEM((1024, 128), F32)],
        compiler_params=params(2, 60),
        cost_estimate=cost(1 << 30, 10 * mega),
        name="front",
    )(layer, pre, slope_in)
    arrived = exchange(message, PLANE)

    blocks = np.kron(np.eye(2, dtype=np.float32), np.ones((32, 32), np.float32))
    both = jnp.tile(point_weight, (2, 2)) * blocks
    base, sums = pl.pallas_call(
        local_kernel,
        grid=(2, 2),
        in_specs=[whole(64, 64), field, field, field],
        out_specs=[field, whole(8, 128)],
        out_shape=[shaped(64, 4, 16, 128), shaped(8, 128)],
        scratch_shapes=[pltpu.VMEM((64, 64), F32), pltpu.VMEM((1024, 128), F32)],
        compiler_params=params(2, 60),
        cost_estimate=cost(1 << 30, 8 * mega),
        name="local",
    )(both, layer, pre, slope_in)

    spread = np.kron(np.eye(64, dtype=np.float32), np.ones((1, 32), np.float32))
    column = pl.BlockSpec((128, 512), lambda i: (0, i))
    codes, _ = lax.optimization_barrier((weight_codes, sums))
    weight = pl.pallas_call(
        weight_kernel,
        grid=(4,),
        in_specs=[pl.BlockSpec((64, 512), lambda i: (0, i)), column, whole(128, 64), column],
        out_specs=column,
        out_shape=shaped(128, 2048),
        compiler_params=params(1),
        cost_estimate=cost(1 << 27, 3 * mega),
        name="weight",
    )(
        jnp.asarray(spread, BF16),
        codes.reshape(128, 2048),
        scale_codes.reshape(128, 64),
        weight_noise.reshape(128, 2048),
    )

    def placed(in_specs, out_specs, scratch=()):
        return pltpu.PrefetchScalarGridSpec(
            num_scalar_prefetch=1,
            grid=(1,),
            in_specs=in_specs,
            out_specs=out_specs,
            scratch_shapes=scratch,
        )

    def one_field(index):
        return pl.BlockSpec((16, 1, 2, 64, 128), lambda *_: (0, index, 0, 0, 0))

    message = pl.pallas_call(
        x_kernel,
        grid_spec=placed([one_field(1), whole(8, 128)], whole(16, 9, 8, 128)),
        out_shape=shaped(16, 9, 8, 128),
        compiler_params=params(1),
        cost_estimate=cost(1 << 29, 2 * mega),
        name="x_modes",
    )(place, arrived, sums)
    keep, give = pl.pallas_call(
        x_side_kernel,
        grid_spec=placed(
            [one_field(0)], [whole(8, 8, 8, 128)] * 2, [pltpu.VMEM((16, 8, 8, 128), F32)]
        ),
        out_shape=[shaped(8, 8, 8, 128)] * 2,
        compiler_params=params(1),
        cost_estimate=cost(1 << 29, 2 * mega),
        name="x_side",
    )(place, arrived)
    arrived = exchange(message, COLUMN)
    got = lax.ppermute(give, "co", [(0, 1), (1, 0)])
    pairs = pl.pallas_call(
        pair_kernel,
        grid=(1,),
        in_specs=[whole(8, 8, 8, 128)] * 2,
        out_specs=[whole(2, 8, 8, 128)] * 8,
        out_shape=[shaped(2, 8, 8, 128)] * 8,
        compiler_params=params(1),
        cost_estimate=cost(1 << 20, mega),
        name="pair",
    )(keep, got)

    def hop(step):
        route = [(chip, (chip + step) % 8) for chip in range(8)]
        return lax.ppermute(pairs[step], ("zh", "zl"), route)

    sent = {0: pairs[0]}
    sent.update((step, hop(step)) for step in ())
    weight, sent, pairs = lax.optimization_barrier((weight, sent, pairs))
    g_hat, message, sums = pl.pallas_call(
        mode_kernel,
        grid_spec=placed(
            [whole(128, 2048), whole(16, 9, 8, 128)],
            [whole(2, 128, 128), whole(16, 8, 8, 128), whole(8, 128)],
        ),
        out_shape=[shaped(2, 128, 128), shaped(16, 8, 8, 128), shaped(8, 128)],
        compiler_params=params(1),
        cost_estimate=cost(1 << 30, 3 * mega),
        name="modes",
    )(place, weight, arrived)
    returned = exchange(message, COLUMN)
    sent.update((step, hop(step)) for step in (1, 7, 2, 6))
    returned, sent = lax.optimization_barrier((returned, sent))

    message = pl.pallas_call(
        x_back_kernel,
        grid_spec=placed([whole(16, 8, 8, 128), whole(8, 128)], whole(16, 17, 8, 128)),
        out_shape=shaped(16, 17, 8, 128),
        compiler_params=params(1),
        cost_estimate=cost(1 << 29, 2 * mega),
        name="x_cells",
    )(place, returned, sums)
    returned = exchange(message, PLANE)

    pairs, _ = lax.optimization_barrier((pairs, message))
    sent.update((step, hop(step)) for step in range(1, 8) if step not in sent)
    grad_spectral = pl.pallas_call(
        outer_kernel,
        grid_spec=placed([whole(2, 8, 8, 128)] * 8 + [whole(2, 128, 128)], whole(128, 2048)),
        out_shape=shaped(128, 2048),
        compiler_params=params(1, 60),
        cost_estimate=cost(1 << 30, 4 * mega),
        name="outer",
    )(place, *(sent[step] for step in range(8)), g_hat)

    grad_input, grad_point, grad_bias = pl.pallas_call(
        end_kernel,
        grid=(2, 2),
        in_specs=[
            pl.BlockSpec((16, 4, 8, 128), lambda p, h: (0, 2 * p + h, 0, 0)),
            pl.BlockSpec((16, 1, 8, 128), lambda p, h: (0, 16, 0, 0)),
            pl.BlockSpec(memory_space=pltpu.HBM),
        ],
        out_specs=[field, whole(32, 32), whole(1, 32)],
        out_shape=[shaped(64, 4, 16, 128), shaped(32, 32), shaped(1, 32)],
        scratch_shapes=[
            pltpu.VMEM((128, 256), F32),
            pltpu.VMEM((4, 64, 2, 8, 128), F32),
            pltpu.SemaphoreType.DMA((4,)),
        ],
        compiler_params=params(2),
        cost_estimate=cost(1 << 29, 5 * mega),
        name="end",
    )(returned, returned, base)
    return (
        grad_input.reshape(layer_input.shape),
        grad_spectral.reshape(weight_codes.shape),
        grad_point,
        grad_bias.reshape(32),
    )


def solution(mesh):
    fine = Mesh(mesh.devices.reshape(4, 2, 4, 4, 2), ("yp", "zh", "xp", "zl", "co"))
    slab, pencil = ("yp", "zh", "xp"), ("zl", "co")
    field, modes = P(None, None, slab, pencil, None), P(slab, pencil, None, None)
    return jax.shard_map(
        per_device,
        mesh=fine,
        in_specs=(field, field, field, modes, modes, modes, P()),
        out_specs=(field, modes, P(), P()),
        check_vma=False,
    )
```

```python
import math

import jax
import jax.numpy as jnp
import numpy as np
from jax import lax
from jax.experimental import pallas as pl
from jax.experimental.pallas import tpu as pltpu
from jax.sharding import Mesh
from jax.sharding import PartitionSpec as P

F32 = jnp.float32
BF16 = jnp.bfloat16
CELLS = 4194304.0
UNIT = 1.0 / math.sqrt(128.0 * 128.0 * 128.0)
PLANE = ("yp", "xp")
COLUMN = ("zh", "zl", "co")


def dot(left, right, left_dim=1, right_dim=0):
    dims = (((left_dim,), (right_dim,)), ((), ()))
    return lax.dot_general(left, right, dims, preferred_element_type=F32)


def halves(values):
    top = values.astype(BF16)
    return top, (values - top.astype(F32)).astype(BF16)


def mm(left, right, left_dim=1, right_dim=0):
    (left_top, left_rest), (right_top, right_rest) = halves(left), halves(right)
    size = left.shape[1 - left_dim]
    both = dot(jnp.concatenate([left_top, left_rest], 1 - left_dim), right_top, left_dim, right_dim)
    return both[:size] + both[size:] + dot(left_top, right_rest, left_dim, right_dim)


def mm_exact(values, pattern):
    top, rest = halves(values)
    return dot(top, pattern) + dot(rest, pattern)


def sine(turns):
    angle = ((turns + 64) & 127) - 64
    angle = jnp.where(angle > 32, 64 - angle, jnp.where(angle < -32, -64 - angle, angle))
    x = angle.astype(F32) * (2.0 * math.pi / 128.0)
    square = x * x
    total = jnp.full_like(x, 1.0 / math.factorial(13))
    for power in (11, 9, 7, 5, 3, 1):
        total = total * square + (-1.0) ** (power // 2) / math.factorial(power)
    return total * x


def grid_of(rows, columns):
    shape = (rows, columns)
    return lax.broadcasted_iota(jnp.int32, shape, 0), lax.broadcasted_iota(jnp.int32, shape, 1)


def z_table(scale):
    row, column = grid_of(128, 256)
    kz = 8 * (row >> 5) + ((row >> 3) & 3) + 4 * (row & 1)
    values = sine(kz * (column & 127) + 32 + 32 * ((row >> 1) & 1))
    return jnp.where(((row >> 2) & 1) == (column >> 7), values * scale, 0.0)


def x_table(zh):
    row, column = grid_of(128, 256)
    cell = 32 * (column >> 6) + 16 * zh + ((column >> 2) & 15)
    quarter = 32 - 32 * (((column >> 1) & 1) - (row & 1))
    values = sine((((row >> 1) & 31) - 16) * cell + quarter)
    return jnp.where((row >> 6) == (column & 1), values, 0.0)


def x_back_table(zh):
    row, column = grid_of(256, 128)
    cell = 32 * (row >> 6) + 16 * zh + ((row >> 2) & 15)
    quarter = 32 + 32 * ((column & 1) - ((row >> 1) & 1))
    values = sine((((column >> 1) & 31) - 16) * cell + quarter)
    return jnp.where((row & 1) == (column >> 6), values, 0.0)


def y_table(pencil_of):
    row, column = grid_of(128, 256)
    cell = 16 * pencil_of((column >> 3) & 15) + 2 * (column & 7) + (row >> 6)
    quarter = 32 - 32 * ((column >> 7) - ((row >> 5) & 1))
    return sine(((row & 31) - 16) * cell + quarter) * UNIT


def y_back_table():
    row, column = grid_of(128, 128)
    cell = 2 * (row & 63) + (column >> 6)
    quarter = 32 + 32 * (((column >> 5) & 1) - (row >> 6))
    return sine(((column & 31) - 16) * cell + quarter)


def pattern(keep):
    return jnp.where(keep, 1.0, 0.0).astype(BF16)


def make_grad(pre, out_grad, grad):
    def some(i, carry):
        rows = pl.ds(pl.multiple_of(i * 64, 64), 64)
        v = pre[rows, :]
        cdf = 0.5 * (1.0 + lax.erf(v * (1.0 / math.sqrt(2.0))))
        bump = v * jnp.exp(-0.5 * v * v) * (1.0 / math.sqrt(2.0 * math.pi))
        grad[rows, :] = out_grad[rows, :] * (cdf + bump)
        return carry

    lax.fori_loop(0, grad.shape[0] // 64, some, 0)


def front_kernel(layer, pre, out_grad, message, table, grad2):
    @pl.when(pl.program_id(0) + pl.program_id(1) == 0)
    def _():
        table[...] = jnp.concatenate(halves(z_table(1.0)), 0)

    layer, pre, out_grad = (ref.reshape(1024, 128) for ref in (layer, pre, out_grad))
    make_grad(pre, out_grad, grad2)
    for field, values in ((0, layer), (1, grad2)):
        for j in range(0, 4, 2):
            cells = [
                jnp.concatenate(
                    [values[pl.ds(x * 8 + 2 * j + y, 64, stride=16), :] for y in range(4)], 0
                )
                for x in range(2)
            ]
            top, rest = halves(jnp.concatenate(cells, 1))
            spectrum = dot(top, table[...], 1, 1)
            spectrum = spectrum[:, :128] + spectrum[:, 128:] + dot(rest, table[:128], 1, 1)
            spectrum = spectrum.T
            for k in range(2):
                part = spectrum[:, 128 * k : 128 * k + 128].reshape(16, 8, 128)
                message[:, field, 0, 8 * (j + k) : 8 * (j + k) + 8, :] = part


def local_kernel(point, layer, pre, out_grad, base, sums, products, grad):
    layer, pre, out_grad, base = (ref.reshape(1024, 128) for ref in (layer, pre, out_grad, base))
    make_grad(pre, out_grad, grad)
    step = pl.program_id(0) * 2 + pl.program_id(1)

    @pl.when(step == 0)
    def _():
        products[...] = jnp.zeros_like(products)

    for cell in range(0, 16, 2):
        u = jnp.concatenate([layer[pl.ds(cell + k, 64, stride=16), :] for k in range(2)], 1)
        g = jnp.concatenate([grad[pl.ds(cell + k, 64, stride=16), :] for k in range(2)], 1)
        products[...] += mm(u, g, 1, 1)
        mixed = mm(point[...], g)
        for k in range(2):
            base[pl.ds(cell + k, 64, stride=16), :] = mixed[:, 128 * k : 128 * k + 128]

    @pl.when(step == 3)
    def _():
        by_pair = products[0:32, 0:32] + products[32:64, 32:64]
        for k in range(4):
            sums[:, 32 * k : 32 * k + 32] = by_pair[8 * k : 8 * k + 8, :]


def weight_kernel(spread, codes, scales, noise, weight):
    step = jnp.exp2(scales[...].astype(F32) * -0.25) * (1.0 / (16.0 * math.sqrt(32.0)))
    top, rest = halves(step)
    last = (step - top.astype(F32) - rest.astype(F32)).astype(BF16)
    wide = sum(dot(part, spread[...]) for part in (last, rest, top))
    weight[...] = codes[...].astype(F32) * wide * (1.0 + noise[...])


def along_x(table, arrived, j):
    cells = [arrived[:, 0, :, 8 * k : 8 * k + 8, :].reshape(256, 128) for k in (j, j + 1)]
    return mm(table, jnp.concatenate(cells, 1))


def x_kernel(place, arrived, sums, message):
    message[:, 8] = jnp.broadcast_to(sums[...][None], (16, 8, 128))
    table = x_table(place[0])
    for j in range(0, 8, 2):
        modes = along_x(table, arrived, j)
        for k in range(2):
            message[:, j + k] = modes[:, 128 * k : 128 * k + 128].reshape(16, 8, 128)


def x_side_kernel(place, arrived, keep, give, tiles):
    table = x_table(place[0])
    for j in range(0, 8, 2):
        modes = along_x(table, arrived, j)
        for k in range(2):
            tiles[:, j + k] = modes[:, 128 * k : 128 * k + 128].reshape(16, 8, 128)
    for step in range(8):
        peer = 2 * ((place[3] + step) & 7)
        keep[step] = tiles[peer + place[4]]
        give[step] = tiles[peer + 1 - place[4]]


def pair_kernel(keep, got, *pairs):
    for step, pair in enumerate(pairs):
        pair[0] = keep[step]
        pair[1] = got[step]


def along_y(table, pieces):
    cells = [
        jnp.concatenate(
            [rows[pl.ds(at + 2 * kx + r, 8, stride=8), :] for r in range(2) for rows, at in pieces], 0
        )
        for kx in range(4)
    ]
    modes = mm(table, jnp.concatenate(cells, 1))
    modes = [modes[:, 128 * kx : 128 * kx + 128] for kx in range(4)]
    modes = [part[:64] + pltpu.roll(part[64:], 64, 1) for part in modes]
    real, imag = ([part[32 * r : 32 * r + 32] for part in modes] for r in range(2))
    return jnp.concatenate(real, 0), jnp.concatenate(imag, 0)


def mode_kernel(place, weight, arrived, g_there, message, sums, g_hat, sent):
    sums[...] = jnp.sum(arrived[:, 8], axis=0)
    sources = arrived.reshape(1152, 128)
    table = y_table(lambda source: source & 7)
    g_real, g_imag = along_y(table, [(sources, 72 * peer) for peer in range(16)])
    g_hat[0] = g_real
    g_hat[1] = g_imag
    store = pltpu.make_async_copy(g_hat, g_there, sent)
    store.start()
    row, column = grid_of(128, 128)
    row_long, column_long = grid_of(1024, 128)
    gather = pattern((row_long >> 5) == column_long)
    q_real = q_imag = None
    for b in range(2):
        wide = pattern(row == (column & 31) + 32 * b)
        wide_real, wide_imag = mm_exact(g_real, wide), mm_exact(g_imag, wide)
        real = imag = 0.0
        for part in range(4):
            lanes = slice(256 * part, 256 * part + 256)
            w_real = weight[:, 256 * part : 256 * part + 256]
            w_imag = weight[:, 1024 + 256 * part : 1280 + 256 * part]
            gr = jnp.concatenate([wide_real, wide_real], 1)
            gi = jnp.concatenate([wide_imag, wide_imag], 1)
            real += mm_exact(w_real * gr + w_imag * gi, gather[lanes])
            imag += mm_exact(w_real * gi - w_imag * gr, gather[lanes])
        if b == 0:
            q_real, q_imag = real, imag
        else:
            q_real, q_imag = q_real + pltpu.roll(real, 32, 1), q_imag + pltpu.roll(imag, 32, 1)
    rows = message.reshape(1024, 128)
    modes = [
        jnp.concatenate([q_real[32 * kx : 32 * kx + 32], q_imag[32 * kx : 32 * kx + 32]], 0)
        for kx in range(4)
    ]
    modes = [jnp.concatenate([part, pltpu.roll(part, 64, 1)], 0) for part in modes]
    cells = mm(y_back_table(), jnp.concatenate(modes, 1))
    for kx in range(4):
        for r in range(2):
            for zh in range(2):
                part = cells[64 * r : 64 * r + 64, 128 * kx : 128 * kx + 128]
                rows[pl.ds(512 * zh + 2 * kx + r, 64, stride=8), :] = part

    @pl.when(place[2] == 1)
    def _():
        bias = g_real[16:17] + pltpu.roll(g_real[16:17], 96, 1)
        rows[pl.ds(1, 16, stride=64), :] = jnp.broadcast_to(bias * (1.0 / (UNIT * CELLS)), (16, 128))

    store.wait()


def outer_kernel(place, *refs):
    *pairs, g_hat, result = refs

    def pencil(source):
        return 2 * ((place[3] - (source >> 1)) & 3) + ((source & 1) ^ place[4])

    pieces = [(pair.reshape(128, 128), 64 * k) for pair in pairs for k in range(2)]
    u_real, u_imag = along_y(y_table(pencil), pieces)
    row, column = grid_of(128, 128)
    u, g = [], []
    for b in range(2):
        wide = pattern(row == (column & 31) + 32 * b)
        u.append([pltpu.roll(v, 96, 1) if b else v for v in (u_real, u_imag)])
        g.append([mm_exact(g_hat[r], wide) for r in range(2)])
    g = [[jnp.concatenate([v, v], 1) for v in pair] for pair in g]
    row, column = grid_of(128, 256)
    for part in range(4):
        wide = pattern(row == (column >> 5) + 8 * part)
        real = imag = 0.0
        for b in range(2):
            ur, ui = (mm_exact(v, wide) for v in u[b])
            gr, gi = g[b]
            real += ur * gr + ui * gi
            imag += ur * gi - ui * gr
        result[:, 256 * part : 256 * part + 256] = real
        result[:, 1024 + 256 * part : 1280 + 256 * part] = imag


def x_back_kernel(place, arrived, sums, message):
    message[:, 16] = jnp.broadcast_to(sums[...][None], (16, 8, 128))
    table = x_back_table(place[0])
    for j in range(0, 8, 2):
        cells = jnp.concatenate([arrived[:, k].reshape(128, 128) for k in (j, j + 1)], 1)
        cells = mm(table, cells)
        for k in range(2):
            part = cells[:, 128 * k : 128 * k + 128].reshape(16, 2, 8, 128)
            message[:, j + k] = part[:, 0]
            message[:, 8 + j + k] = part[:, 1]

    @pl.when(place[1] == 1)
    def _():
        message[:, 0, 2:3] = jnp.broadcast_to(arrived[4, 0, 1:2][None], (16, 1, 128))


def end_kernel(arrived, sums, base, result, grad_point, grad_bias, table, held, taken):
    result = result.reshape(1024, 128)
    step = 2 * pl.program_id(0) + pl.program_id(1)

    def load(n):
        there = base.at[:, pl.ds(2 * (n // 2), 2), pl.ds(8 * (n % 2), 8), :]
        return pltpu.make_async_copy(there, held.at[n], taken.at[n])

    @pl.when(step == 0)
    def _():
        for n in range(4):
            load(n).start()
        table[...] = z_table(UNIT)
        total = jnp.sum(sums[:, 0], axis=0) * (1.0 / CELLS)
        for k in range(4):
            grad_point[8 * k : 8 * k + 8, :] = total[:, 32 * k : 32 * k + 32]
        grad_bias[...] = arrived[0, 0, 2:3, 0:32]

    for n in range(4):

        @pl.when(step == n)
        def _():
            load(n).wait()
            rest = held.at[n].reshape(1024, 128)
            for j in range(4):
                cells = mm(arrived[:, j].reshape(128, 128), table[...], 0, 0)
                for x in range(2):
                    for odd in range(2):
                        rows = pl.ds(x * 8 + 2 * j + odd, 64, stride=16)
                        part = cells[64 * odd : 64 * odd + 64, 128 * x : 128 * x + 128]
                        result[rows, :] = rest[rows, :] + part


def params(steps=0, mebibytes=20):
    return pltpu.CompilerParams(
        dimension_semantics=("arbitrary",) * steps if steps else None,
        vmem_limit_bytes=mebibytes << 20,
    )


def cost(flops, moved):
    return pl.CostEstimate(flops=flops, bytes_accessed=moved, transcendentals=0)


def whole(*shape):
    return pl.BlockSpec(shape, lambda *_: (0,) * len(shape))


def shaped(*shape):
    return jax.ShapeDtypeStruct(shape, F32)


def exchange(message, axes):
    return lax.all_to_all(message, axes, split_axis=0, concat_axis=0, tiled=True)


def per_device(
    layer_input, pre_act, out_grad, weight_codes, scale_codes, weight_noise, point_weight
):
    layer, pre, slope_in = (v.reshape(64, 4, 16, 128) for v in (layer_input, pre_act, out_grad))
    plane_first = (lax.axis_index("yp") + lax.axis_index("xp") == 0).astype(jnp.int32)
    owner = plane_first * (lax.axis_index(COLUMN) == 4).astype(jnp.int32)
    chip, core = lax.axis_index(("zh", "zl")), lax.axis_index("co")
    place = jnp.stack([lax.axis_index("zh"), plane_first, owner, chip, core]).astype(jnp.int32)
    mega = 1 << 20
    field = pl.BlockSpec((64, 2, 8, 128), lambda p, h: (0, p, h, 0))
    message = pl.pallas_call(
        front_kernel,
        grid=(2, 2),
        in_specs=[field, field, field],
        out_specs=pl.BlockSpec((16, 2, 1, 32, 128), lambda p, h: (0, 0, p, h, 0)),
        out_shape=shaped(16, 2, 2, 64, 128),
        scratch_shapes=[pltpu.VMEM((256, 256), BF16), pltpu.VMEM((1024, 128), F32)],
        compiler_params=params(2, 60),
        cost_estimate=cost(1 << 30, 10 * mega),
        name="front",
    )(layer, pre, slope_in)
    arrived = exchange(message, PLANE)

    blocks = np.kron(np.eye(2, dtype=np.float32), np.ones((32, 32), np.float32))
    both = jnp.tile(point_weight, (2, 2)) * blocks
    base, sums = pl.pallas_call(
        local_kernel,
        grid=(2, 2),
        in_specs=[whole(64, 64), field, field, field],
        out_specs=[field, whole(8, 128)],
        out_shape=[shaped(64, 4, 16, 128), shaped(8, 128)],
        scratch_shapes=[pltpu.VMEM((64, 64), F32), pltpu.VMEM((1024, 128), F32)],
        compiler_params=params(2),
        cost_estimate=cost(1 << 30, 8 * mega),
        name="local",
    )(both, layer, pre, slope_in)

    spread = np.kron(np.eye(64, dtype=np.float32), np.ones((1, 32), np.float32))
    column = pl.BlockSpec((128, 512), lambda i: (0, i))
    codes, _ = lax.optimization_barrier((weight_codes, sums))
    weight = pl.pallas_call(
        weight_kernel,
        grid=(4,),
        in_specs=[pl.BlockSpec((64, 512), lambda i: (0, i)), column, whole(128, 64), column],
        out_specs=column,
        out_shape=shaped(128, 2048),
        compiler_params=params(1),
        cost_estimate=cost(1 << 27, 3 * mega),
        name="weight",
    )(
        jnp.asarray(spread, BF16),
        codes.reshape(128, 2048),
        scale_codes.reshape(128, 64),
        weight_noise.reshape(128, 2048),
    )

    def placed(in_specs, out_specs, scratch=()):
        return pltpu.PrefetchScalarGridSpec(
            num_scalar_prefetch=1,
            grid=(1,),
            in_specs=in_specs,
            out_specs=out_specs,
            scratch_shapes=scratch,
        )

    in_hbm = pl.BlockSpec(memory_space=pltpu.HBM)

    def one_field(index):
        return pl.BlockSpec((16, 1, 2, 64, 128), lambda *_: (0, index, 0, 0, 0))

    message = pl.pallas_call(
        x_kernel,
        grid_spec=placed([one_field(1), whole(8, 128)], whole(16, 9, 8, 128)),
        out_shape=shaped(16, 9, 8, 128),
        compiler_params=params(1),
        cost_estimate=cost(1 << 29, 2 * mega),
        name="x_modes",
    )(place, arrived, sums)
    keep, give = pl.pallas_call(
        x_side_kernel,
        grid_spec=placed(
            [one_field(0)], [whole(8, 8, 8, 128)] * 2, [pltpu.VMEM((16, 8, 8, 128), F32)]
        ),
        out_shape=[shaped(8, 8, 8, 128)] * 2,
        compiler_params=params(1),
        cost_estimate=cost(1 << 29, 2 * mega),
        name="x_side",
    )(place, arrived)
    arrived = exchange(message, COLUMN)
    got = lax.ppermute(give, "co", [(0, 1), (1, 0)])
    pairs = pl.pallas_call(
        pair_kernel,
        grid=(1,),
        in_specs=[whole(8, 8, 8, 128)] * 2,
        out_specs=[whole(2, 8, 8, 128)] * 8,
        out_shape=[shaped(2, 8, 8, 128)] * 8,
        compiler_params=params(1),
        cost_estimate=cost(1 << 20, mega),
        name="pair",
    )(keep, got)

    def hop(step):
        route = [(chip, (chip + step) % 8) for chip in range(8)]
        return lax.ppermute(pairs[step], ("zh", "zl"), route)

    sent = {0: pairs[0]}
    weight, sent, pairs = lax.optimization_barrier((weight, sent, pairs))
    g_hat, message, sums = pl.pallas_call(
        mode_kernel,
        grid_spec=placed(
            [whole(128, 2048), whole(16, 9, 8, 128)],
            [in_hbm, whole(16, 8, 8, 128), whole(8, 128)],
            [pltpu.VMEM((2, 128, 128), F32), pltpu.SemaphoreType.DMA],
        ),
        out_shape=[shaped(2, 128, 128), shaped(16, 8, 8, 128), shaped(8, 128)],
        compiler_params=params(1),
        cost_estimate=cost(1 << 30, 3 * mega),
        name="modes",
    )(place, weight, arrived)
    returned = exchange(message, COLUMN)
    sent.update((step, hop(step)) for step in (1,7,2,6))
    returned, sent = lax.optimization_barrier((returned, sent))

    message = pl.pallas_call(
        x_back_kernel,
        grid_spec=placed([whole(16, 8, 8, 128), whole(8, 128)], whole(16, 17, 8, 128)),
        out_shape=shaped(16, 17, 8, 128),
        compiler_params=params(1),
        cost_estimate=cost(1 << 29, 2 * mega),
        name="x_cells",
    )(place, returned, sums)
    returned = exchange(message, PLANE)

    pairs, _ = lax.optimization_barrier((pairs, message))
    sent.update((step, hop(step)) for step in range(1, 8) if step not in sent)
    grad_spectral = pl.pallas_call(
        outer_kernel,
        grid_spec=placed([whole(2, 8, 8, 128)] * 8 + [whole(2, 128, 128)], whole(128, 2048)),
        out_shape=shaped(128, 2048),
        compiler_params=params(1, 60),
        cost_estimate=cost(1 << 30, 4 * mega),
        name="outer",
    )(place, *(sent[step] for step in range(8)), g_hat)

    grad_input, grad_point, grad_bias = pl.pallas_call(
        end_kernel,
        grid=(2, 2),
        in_specs=[
            pl.BlockSpec((16, 4, 8, 128), lambda p, h: (0, 2 * p + h, 0, 0)),
            pl.BlockSpec((16, 1, 8, 128), lambda p, h: (0, 16, 0, 0)),
            in_hbm,
        ],
        out_specs=[field, whole(32, 32), whole(1, 32)],
        out_shape=[shaped(64, 4, 16, 128), shaped(32, 32), shaped(1, 32)],
        scratch_shapes=[
            pltpu.VMEM((128, 256), F32),
            pltpu.VMEM((4, 64, 2, 8, 128), F32),
            pltpu.SemaphoreType.DMA((4,)),
        ],
        compiler_params=params(2),
        cost_estimate=cost(1 << 29, 5 * mega),
        name="end",
    )(returned, returned, base)
    return (
        grad_input.reshape(layer_input.shape),
        grad_spectral.reshape(weight_codes.shape),
        grad_point,
        grad_bias.reshape(32),
    )


def solution(mesh):
    fine = Mesh(mesh.devices.reshape(4, 2, 4, 4, 2), ("yp", "zh", "xp", "zl", "co"))
    slab, pencil = ("yp", "zh", "xp"), ("zl", "co")
    field, modes = P(None, None, slab, pencil, None), P(slab, pencil, None, None)
    return jax.shard_map(
        per_device,
        mesh=fine,
        in_specs=(field, field, field, modes, modes, modes, P()),
        out_specs=(field, modes, P(), P()),
        check_vma=False,
    )
```

```python
import math

import jax
import jax.numpy as jnp
import numpy as np
from jax import lax
from jax.experimental import pallas as pl
from jax.experimental.pallas import tpu as pltpu
from jax.sharding import Mesh
from jax.sharding import PartitionSpec as P

F32 = jnp.float32
BF16 = jnp.bfloat16
CELLS = 4194304.0
UNIT = 1.0 / math.sqrt(128.0 * 128.0 * 128.0)
PLANE = ("yp", "xp")
COLUMN = ("zh", "zl", "co")


def dot(left, right, left_dim=1, right_dim=0):
    dims = (((left_dim,), (right_dim,)), ((), ()))
    return lax.dot_general(left, right, dims, preferred_element_type=F32)


def halves(values):
    top = values.astype(BF16)
    return top, (values - top.astype(F32)).astype(BF16)


def mm(left, right, left_dim=1, right_dim=0):
    (left_top, left_rest), (right_top, right_rest) = halves(left), halves(right)
    size = left.shape[1 - left_dim]
    both = dot(jnp.concatenate([left_top, left_rest], 1 - left_dim), right_top, left_dim, right_dim)
    return both[:size] + both[size:] + dot(left_top, right_rest, left_dim, right_dim)


def mm_exact(values, pattern):
    top, rest = halves(values)
    return dot(top, pattern) + dot(rest, pattern)


def sine(turns):
    angle = ((turns + 64) & 127) - 64
    angle = jnp.where(angle > 32, 64 - angle, jnp.where(angle < -32, -64 - angle, angle))
    x = angle.astype(F32) * (2.0 * math.pi / 128.0)
    square = x * x
    total = jnp.full_like(x, 1.0 / math.factorial(13))
    for power in (11, 9, 7, 5, 3, 1):
        total = total * square + (-1.0) ** (power // 2) / math.factorial(power)
    return total * x


def grid_of(rows, columns):
    shape = (rows, columns)
    return lax.broadcasted_iota(jnp.int32, shape, 0), lax.broadcasted_iota(jnp.int32, shape, 1)


def z_table(scale):
    row, column = grid_of(128, 256)
    kz = 8 * (row >> 5) + ((row >> 3) & 3) + 4 * (row & 1)
    values = sine(kz * (column & 127) + 32 + 32 * ((row >> 1) & 1))
    return jnp.where(((row >> 2) & 1) == (column >> 7), values * scale, 0.0)


def x_table(zh):
    row, column = grid_of(128, 256)
    cell = 32 * (column >> 6) + 16 * zh + ((column >> 2) & 15)
    quarter = 32 - 32 * (((column >> 1) & 1) - (row & 1))
    values = sine((((row >> 1) & 31) - 16) * cell + quarter)
    return jnp.where((row >> 6) == (column & 1), values, 0.0)


def x_back_table(zh):
    row, column = grid_of(256, 128)
    cell = 32 * (row >> 6) + 16 * zh + ((row >> 2) & 15)
    quarter = 32 + 32 * ((column & 1) - ((row >> 1) & 1))
    values = sine((((column >> 1) & 31) - 16) * cell + quarter)
    return jnp.where((row & 1) == (column >> 6), values, 0.0)


def y_table(pencil_of):
    row, column = grid_of(128, 256)
    cell = 16 * pencil_of((column >> 3) & 15) + 2 * (column & 7) + (row >> 6)
    quarter = 32 - 32 * ((column >> 7) - ((row >> 5) & 1))
    return sine(((row & 31) - 16) * cell + quarter) * UNIT


def y_back_table():
    row, column = grid_of(128, 128)
    cell = 2 * (row & 63) + (column >> 6)
    quarter = 32 + 32 * (((column >> 5) & 1) - (row >> 6))
    return sine(((column & 31) - 16) * cell + quarter)


def pattern(keep):
    return jnp.where(keep, 1.0, 0.0).astype(BF16)


def make_grad(pre, out_grad, grad):
    def some(i, carry):
        rows = pl.ds(pl.multiple_of(i * 64, 64), 64)
        v = pre[rows, :]
        cdf = 0.5 * (1.0 + lax.erf(v * (1.0 / math.sqrt(2.0))))
        bump = v * jnp.exp(-0.5 * v * v) * (1.0 / math.sqrt(2.0 * math.pi))
        grad[rows, :] = out_grad[rows, :] * (cdf + bump)
        return carry

    lax.fori_loop(0, grad.shape[0] // 64, some, 0)


def front_kernel(layer, pre, out_grad, message, table, grad2):
    @pl.when(pl.program_id(0) + pl.program_id(1) == 0)
    def _():
        table[...] = jnp.concatenate(halves(z_table(1.0)), 0)

    layer, pre, out_grad = (ref.reshape(1024, 128) for ref in (layer, pre, out_grad))
    make_grad(pre, out_grad, grad2)
    for field, values in ((0, layer), (1, grad2)):
        for j in range(0, 4, 2):
            cells = [
                jnp.concatenate(
                    [values[pl.ds(x * 8 + 2 * j + y, 64, stride=16), :] for y in range(4)], 0
                )
                for x in range(2)
            ]
            top, rest = halves(jnp.concatenate(cells, 1))
            spectrum = dot(top, table[...], 1, 1)
            spectrum = spectrum[:, :128] + spectrum[:, 128:] + dot(rest, table[:128], 1, 1)
            spectrum = spectrum.T
            for k in range(2):
                part = spectrum[:, 128 * k : 128 * k + 128].reshape(16, 8, 128)
                message[:, field, 0, 8 * (j + k) : 8 * (j + k) + 8, :] = part


def local_kernel(point, layer, pre, out_grad, base, sums, products, grad):
    layer, pre, out_grad, base = (ref.reshape(1024, 128) for ref in (layer, pre, out_grad, base))
    make_grad(pre, out_grad, grad)
    step = pl.program_id(0) * 2 + pl.program_id(1)

    @pl.when(step == 0)
    def _():
        products[...] = jnp.zeros_like(products)

    for cell in range(0, 16, 2):
        u = jnp.concatenate([layer[pl.ds(cell + k, 64, stride=16), :] for k in range(2)], 1)
        g = jnp.concatenate([grad[pl.ds(cell + k, 64, stride=16), :] for k in range(2)], 1)
        products[...] += mm(u, g, 1, 1)
        mixed = mm(point[...], g)
        for k in range(2):
            base[pl.ds(cell + k, 64, stride=16), :] = mixed[:, 128 * k : 128 * k + 128]

    @pl.when(step == 3)
    def _():
        by_pair = products[0:32, 0:32] + products[32:64, 32:64]
        for k in range(4):
            sums[:, 32 * k : 32 * k + 32] = by_pair[8 * k : 8 * k + 8, :]


def weight_kernel(spread, codes, scales, noise, weight):
    step = jnp.exp2(scales[...].astype(F32) * -0.25) * (1.0 / (16.0 * math.sqrt(32.0)))
    top, rest = halves(step)
    last = (step - top.astype(F32) - rest.astype(F32)).astype(BF16)
    wide = sum(dot(part, spread[...]) for part in (last, rest, top))
    weight[...] = codes[...].astype(F32) * wide * (1.0 + noise[...])


def along_x(table, arrived, j):
    cells = [arrived[:, 0, :, 8 * k : 8 * k + 8, :].reshape(256, 128) for k in (j, j + 1)]
    return mm(table, jnp.concatenate(cells, 1))


def x_kernel(place, arrived, message):
    table = x_table(place[0])
    for j in range(0, 8, 2):
        modes = along_x(table, arrived, j)
        for k in range(2):
            message[:, j + k] = modes[:, 128 * k : 128 * k + 128].reshape(16, 8, 128)


def x_side_kernel(place, arrived, keep, give, tiles):
    table = x_table(place[0])
    for j in range(0, 8, 2):
        modes = along_x(table, arrived, j)
        for k in range(2):
            tiles[:, j + k] = modes[:, 128 * k : 128 * k + 128].reshape(16, 8, 128)
    for step in range(8):
        peer = 2 * ((place[3] + step) & 7)
        keep[step] = tiles[peer + place[4]]
        give[step] = tiles[peer + 1 - place[4]]


def pair_kernel(keep, got, *pairs):
    for step, pair in enumerate(pairs):
        pair[0] = keep[step]
        pair[1] = got[step]


def along_y(table, pieces):
    cells = [
        jnp.concatenate(
            [rows[pl.ds(at + 2 * kx + r, 8, stride=8), :] for r in range(2) for rows, at in pieces], 0
        )
        for kx in range(4)
    ]
    modes = mm(table, jnp.concatenate(cells, 1))
    modes = [modes[:, 128 * kx : 128 * kx + 128] for kx in range(4)]
    modes = [part[:64] + pltpu.roll(part[64:], 64, 1) for part in modes]
    real, imag = ([part[32 * r : 32 * r + 32] for part in modes] for r in range(2))
    return jnp.concatenate(real, 0), jnp.concatenate(imag, 0)


def mode_kernel(place, weight, arrived, g_there, message, g_hat, sent):
    sources = arrived.reshape(1024, 128)
    table = y_table(lambda source: source & 7)
    g_real, g_imag = along_y(table, [(sources, 64 * peer) for peer in range(16)])
    g_hat[0] = g_real
    g_hat[1] = g_imag
    store = pltpu.make_async_copy(g_hat, g_there, sent)
    store.start()
    row, column = grid_of(128, 128)
    row_long, column_long = grid_of(1024, 128)
    gather = pattern((row_long >> 5) == column_long)
    q_real = q_imag = None
    for b in range(2):
        wide = pattern(row == (column & 31) + 32 * b)
        wide_real, wide_imag = mm_exact(g_real, wide), mm_exact(g_imag, wide)
        real = imag = 0.0
        for part in range(4):
            lanes = slice(256 * part, 256 * part + 256)
            w_real = weight[:, 256 * part : 256 * part + 256]
            w_imag = weight[:, 1024 + 256 * part : 1280 + 256 * part]
            gr = jnp.concatenate([wide_real, wide_real], 1)
            gi = jnp.concatenate([wide_imag, wide_imag], 1)
            real += mm_exact(w_real * gr + w_imag * gi, gather[lanes])
            imag += mm_exact(w_real * gi - w_imag * gr, gather[lanes])
        if b == 0:
            q_real, q_imag = real, imag
        else:
            q_real, q_imag = q_real + pltpu.roll(real, 32, 1), q_imag + pltpu.roll(imag, 32, 1)
    rows = message.reshape(1024, 128)
    modes = [
        jnp.concatenate([q_real[32 * kx : 32 * kx + 32], q_imag[32 * kx : 32 * kx + 32]], 0)
        for kx in range(4)
    ]
    modes = [jnp.concatenate([part, pltpu.roll(part, 64, 1)], 0) for part in modes]
    cells = mm(y_back_table(), jnp.concatenate(modes, 1))
    for kx in range(4):
        for r in range(2):
            for zh in range(2):
                part = cells[64 * r : 64 * r + 64, 128 * kx : 128 * kx + 128]
                rows[pl.ds(512 * zh + 2 * kx + r, 64, stride=8), :] = part

    @pl.when(place[2] == 1)
    def _():
        bias = g_real[16:17] + pltpu.roll(g_real[16:17], 96, 1)
        rows[pl.ds(1, 16, stride=64), :] = jnp.broadcast_to(bias * (1.0 / (UNIT * CELLS)), (16, 128))

    store.wait()


def outer_kernel(place, *refs):
    *pairs, g_hat, result = refs

    def pencil(source):
        return 2 * ((place[3] - (source >> 1)) & 3) + ((source & 1) ^ place[4])

    pieces = [(pair.reshape(128, 128), 64 * k) for pair in pairs for k in range(2)]
    u_real, u_imag = along_y(y_table(pencil), pieces)
    row, column = grid_of(128, 128)
    u, g = [], []
    for b in range(2):
        wide = pattern(row == (column & 31) + 32 * b)
        u.append([pltpu.roll(v, 96, 1) if b else v for v in (u_real, u_imag)])
        g.append([mm_exact(g_hat[r], wide) for r in range(2)])
    g = [[jnp.concatenate([v, v], 1) for v in pair] for pair in g]
    row, column = grid_of(128, 256)
    for part in range(4):
        wide = pattern(row == (column >> 5) + 8 * part)
        real = imag = 0.0
        for b in range(2):
            ur, ui = (mm_exact(v, wide) for v in u[b])
            gr, gi = g[b]
            real += ur * gr + ui * gi
            imag += ur * gi - ui * gr
        result[:, 256 * part : 256 * part + 256] = real
        result[:, 1024 + 256 * part : 1280 + 256 * part] = imag


def x_back_kernel(place, arrived, sums, message):
    message[:, 16] = jnp.broadcast_to(sums[...][None], (16, 8, 128))
    table = x_back_table(place[0])
    for j in range(0, 8, 2):
        cells = jnp.concatenate([arrived[:, k].reshape(128, 128) for k in (j, j + 1)], 1)
        cells = mm(table, cells)
        for k in range(2):
            part = cells[:, 128 * k : 128 * k + 128].reshape(16, 2, 8, 128)
            message[:, j + k] = part[:, 0]
            message[:, 8 + j + k] = part[:, 1]

    @pl.when(place[1] == 1)
    def _():
        message[:, 0, 2:3] = jnp.broadcast_to(arrived[4, 0, 1:2][None], (16, 1, 128))


def end_kernel(arrived, sums, base, result, grad_point, grad_bias, table, held, taken):
    result = result.reshape(1024, 128)
    step = 2 * pl.program_id(0) + pl.program_id(1)

    def load(n):
        there = base.at[:, pl.ds(2 * (n // 2), 2), pl.ds(8 * (n % 2), 8), :]
        return pltpu.make_async_copy(there, held.at[n], taken.at[n])

    @pl.when(step == 0)
    def _():
        for n in range(4):
            load(n).start()
        table[...] = z_table(UNIT)
        total = jnp.sum(sums[:, 0], axis=0) * (1.0 / CELLS)
        for k in range(4):
            grad_point[8 * k : 8 * k + 8, :] = total[:, 32 * k : 32 * k + 32]
        grad_bias[...] = arrived[0, 0, 2:3, 0:32]

    for n in range(4):

        @pl.when(step == n)
        def _():
            load(n).wait()
            rest = held.at[n].reshape(1024, 128)
            for j in range(4):
                cells = mm(arrived[:, j].reshape(128, 128), table[...], 0, 0)
                for x in range(2):
                    for odd in range(2):
                        rows = pl.ds(x * 8 + 2 * j + odd, 64, stride=16)
                        part = cells[64 * odd : 64 * odd + 64, 128 * x : 128 * x + 128]
                        result[rows, :] = rest[rows, :] + part


def params(steps=0, mebibytes=20):
    return pltpu.CompilerParams(
        dimension_semantics=("arbitrary",) * steps if steps else None,
        vmem_limit_bytes=mebibytes << 20,
    )


def cost(flops, moved):
    return pl.CostEstimate(flops=flops, bytes_accessed=moved, transcendentals=0)


def whole(*shape):
    return pl.BlockSpec(shape, lambda *_: (0,) * len(shape))


def shaped(*shape):
    return jax.ShapeDtypeStruct(shape, F32)


def exchange(message, axes):
    return lax.all_to_all(message, axes, split_axis=0, concat_axis=0, tiled=True)


def per_device(
    layer_input, pre_act, out_grad, weight_codes, scale_codes, weight_noise, point_weight
):
    layer, pre, slope_in = (v.reshape(64, 4, 16, 128) for v in (layer_input, pre_act, out_grad))
    plane_first = (lax.axis_index("yp") + lax.axis_index("xp") == 0).astype(jnp.int32)
    owner = plane_first * (lax.axis_index(COLUMN) == 4).astype(jnp.int32)
    chip, core = lax.axis_index(("zh", "zl")), lax.axis_index("co")
    place = jnp.stack([lax.axis_index("zh"), plane_first, owner, chip, core]).astype(jnp.int32)
    mega = 1 << 20
    field = pl.BlockSpec((64, 2, 8, 128), lambda p, h: (0, p, h, 0))
    message = pl.pallas_call(
        front_kernel,
        grid=(2, 2),
        in_specs=[field, field, field],
        out_specs=pl.BlockSpec((16, 2, 1, 32, 128), lambda p, h: (0, 0, p, h, 0)),
        out_shape=shaped(16, 2, 2, 64, 128),
        scratch_shapes=[pltpu.VMEM((256, 256), BF16), pltpu.VMEM((1024, 128), F32)],
        compiler_params=params(2, 60),
        cost_estimate=cost(1 << 30, 10 * mega),
        name="front",
    )(layer, pre, slope_in)
    arrived = exchange(message, PLANE)

    blocks = np.kron(np.eye(2, dtype=np.float32), np.ones((32, 32), np.float32))
    both = jnp.tile(point_weight, (2, 2)) * blocks
    base, sums = pl.pallas_call(
        local_kernel,
        grid=(2, 2),
        in_specs=[whole(64, 64), field, field, field],
        out_specs=[field, whole(8, 128)],
        out_shape=[shaped(64, 4, 16, 128), shaped(8, 128)],
        scratch_shapes=[pltpu.VMEM((64, 64), F32), pltpu.VMEM((1024, 128), F32)],
        compiler_params=params(2, 60),
        cost_estimate=cost(1 << 30, 8 * mega),
        name="local",
    )(both, layer, pre, slope_in)

    for axes, size, bit in (("co", 2, 1), ("zl", 4, 1), ("zl", 4, 2), ("zh", 2, 1)):
        sums = sums + lax.ppermute(sums, axes, [(i, i ^ bit) for i in range(size)])
    arrived, sums = lax.optimization_barrier((arrived, sums))

    spread = np.kron(np.eye(64, dtype=np.float32), np.ones((1, 32), np.float32))
    column = pl.BlockSpec((128, 512), lambda i: (0, i))
    codes, _ = lax.optimization_barrier((weight_codes, sums))
    weight = pl.pallas_call(
        weight_kernel,
        grid=(4,),
        in_specs=[pl.BlockSpec((64, 512), lambda i: (0, i)), column, whole(128, 64), column],
        out_specs=column,
        out_shape=shaped(128, 2048),
        compiler_params=params(1),
        cost_estimate=cost(1 << 27, 3 * mega),
        name="weight",
    )(
        jnp.asarray(spread, BF16),
        codes.reshape(128, 2048),
        scale_codes.reshape(128, 64),
        weight_noise.reshape(128, 2048),
    )

    def placed(in_specs, out_specs, scratch=()):
        return pltpu.PrefetchScalarGridSpec(
            num_scalar_prefetch=1,
            grid=(1,),
            in_specs=in_specs,
            out_specs=out_specs,
            scratch_shapes=scratch,
        )

    in_hbm = pl.BlockSpec(memory_space=pltpu.HBM)

    def one_field(index):
        return pl.BlockSpec((16, 1, 2, 64, 128), lambda *_: (0, index, 0, 0, 0))

    message = pl.pallas_call(
        x_kernel,
        grid_spec=placed([one_field(1)], whole(16, 8, 8, 128)),
        out_shape=shaped(16, 8, 8, 128),
        compiler_params=params(1),
        cost_estimate=cost(1 << 29, 2 * mega),
        name="x_modes",
    )(place, arrived)
    keep, give = pl.pallas_call(
        x_side_kernel,
        grid_spec=placed(
            [one_field(0)], [whole(8, 8, 8, 128)] * 2, [pltpu.VMEM((16, 8, 8, 128), F32)]
        ),
        out_shape=[shaped(8, 8, 8, 128)] * 2,
        compiler_params=params(1),
        cost_estimate=cost(1 << 29, 2 * mega),
        name="x_side",
    )(place, arrived)
    arrived = exchange(message, COLUMN)
    got = lax.ppermute(give, "co", [(0, 1), (1, 0)])
    pairs = pl.pallas_call(
        pair_kernel,
        grid=(1,),
        in_specs=[whole(8, 8, 8, 128)] * 2,
        out_specs=[whole(2, 8, 8, 128)] * 8,
        out_shape=[shaped(2, 8, 8, 128)] * 8,
        compiler_params=params(1),
        cost_estimate=cost(1 << 20, mega),
        name="pair",
    )(keep, got)

    def hop(step):
        route = [(chip, (chip + step) % 8) for chip in range(8)]
        return lax.ppermute(pairs[step], ("zh", "zl"), route)

    sent = {0: pairs[0]}
    weight, sent, pairs = lax.optimization_barrier((weight, sent, pairs))
    g_hat, message = pl.pallas_call(
        mode_kernel,
        grid_spec=placed(
            [whole(128, 2048), whole(16, 8, 8, 128)],
            [in_hbm, whole(16, 8, 8, 128)],
            [pltpu.VMEM((2, 128, 128), F32), pltpu.SemaphoreType.DMA],
        ),
        out_shape=[pltpu.HBM((2, 128, 128), F32), shaped(16, 8, 8, 128)],
        compiler_params=params(1),
        cost_estimate=cost(1 << 30, 3 * mega),
        name="modes",
    )(place, weight, arrived)
    returned = exchange(message, COLUMN)
    sent.update((step, hop(step)) for step in (1,7,2,6))
    returned, sent = lax.optimization_barrier((returned, sent))

    message = pl.pallas_call(
        x_back_kernel,
        grid_spec=placed([whole(16, 8, 8, 128), whole(8, 128)], whole(16, 17, 8, 128)),
        out_shape=shaped(16, 17, 8, 128),
        compiler_params=params(1),
        cost_estimate=cost(1 << 29, 2 * mega),
        name="x_cells",
    )(place, returned, sums)
    returned = exchange(message, PLANE)

    pairs, _ = lax.optimization_barrier((pairs, message))
    sent.update((step, hop(step)) for step in range(1, 8) if step not in sent)
    grad_spectral = pl.pallas_call(
        outer_kernel,
        grid_spec=placed([whole(2, 8, 8, 128)] * 8 + [whole(2, 128, 128)], whole(128, 2048)),
        out_shape=shaped(128, 2048),
        compiler_params=params(1, 60),
        cost_estimate=cost(1 << 30, 4 * mega),
        name="outer",
    )(place, *(sent[step] for step in range(8)), g_hat)

    grad_input, grad_point, grad_bias = pl.pallas_call(
        end_kernel,
        grid=(2, 2),
        in_specs=[
            pl.BlockSpec((16, 4, 8, 128), lambda p, h: (0, 2 * p + h, 0, 0)),
            pl.BlockSpec((16, 1, 8, 128), lambda p, h: (0, 16, 0, 0)),
            in_hbm,
        ],
        out_specs=[field, whole(32, 32), whole(1, 32)],
        out_shape=[shaped(64, 4, 16, 128), shaped(32, 32), shaped(1, 32)],
        scratch_shapes=[
            pltpu.VMEM((128, 256), F32),
            pltpu.VMEM((4, 64, 2, 8, 128), F32),
            pltpu.SemaphoreType.DMA((4,)),
        ],
        compiler_params=params(2),
        cost_estimate=cost(1 << 29, 5 * mega),
        name="end",
    )(returned, returned, base)
    return (
        grad_input.reshape(layer_input.shape),
        grad_spectral.reshape(weight_codes.shape),
        grad_point,
        grad_bias.reshape(32),
    )


def solution(mesh):
    fine = Mesh(mesh.devices.reshape(4, 2, 4, 4, 2), ("yp", "zh", "xp", "zl", "co"))
    slab, pencil = ("yp", "zh", "xp"), ("zl", "co")
    field, modes = P(None, None, slab, pencil, None), P(slab, pencil, None, None)
    return jax.shard_map(
        per_device,
        mesh=fine,
        in_specs=(field, field, field, modes, modes, modes, P()),
        out_specs=(field, modes, P(), P()),
        check_vma=False,
    )
```

```python
import math

import jax
import jax.numpy as jnp
import numpy as np
from jax import lax
from jax.experimental import pallas as pl
from jax.experimental.pallas import tpu as pltpu
from jax.sharding import Mesh
from jax.sharding import PartitionSpec as P

F32 = jnp.float32
BF16 = jnp.bfloat16
CELLS = 4194304.0
UNIT = 1.0 / math.sqrt(128.0 * 128.0 * 128.0)
PLANE = ("yp", "xp")
COLUMN = ("zh", "zl", "co")


def dot(left, right, left_dim=1, right_dim=0):
    dims = (((left_dim,), (right_dim,)), ((), ()))
    return lax.dot_general(left, right, dims, preferred_element_type=F32)


def halves(values):
    top = values.astype(BF16)
    return top, (values - top.astype(F32)).astype(BF16)


def mm(left, right, left_dim=1, right_dim=0):
    (left_top, left_rest), (right_top, right_rest) = halves(left), halves(right)
    size = left.shape[1 - left_dim]
    both = dot(jnp.concatenate([left_top, left_rest], 1 - left_dim), right_top, left_dim, right_dim)
    return both[:size] + both[size:] + dot(left_top, right_rest, left_dim, right_dim)


def mm_exact(values, pattern):
    top, rest = halves(values)
    return dot(top, pattern) + dot(rest, pattern)


def sine(turns):
    angle = ((turns + 64) & 127) - 64
    angle = jnp.where(angle > 32, 64 - angle, jnp.where(angle < -32, -64 - angle, angle))
    x = angle.astype(F32) * (2.0 * math.pi / 128.0)
    square = x * x
    total = jnp.full_like(x, 1.0 / math.factorial(13))
    for power in (11, 9, 7, 5, 3, 1):
        total = total * square + (-1.0) ** (power // 2) / math.factorial(power)
    return total * x


def grid_of(rows, columns):
    shape = (rows, columns)
    return lax.broadcasted_iota(jnp.int32, shape, 0), lax.broadcasted_iota(jnp.int32, shape, 1)


def z_table(scale):
    row, column = grid_of(128, 256)
    kz = 8 * (row >> 5) + ((row >> 3) & 3) + 4 * (row & 1)
    values = sine(kz * (column & 127) + 32 + 32 * ((row >> 1) & 1))
    return jnp.where(((row >> 2) & 1) == (column >> 7), values * scale, 0.0)


def x_table(zh):
    row, column = grid_of(128, 256)
    cell = 32 * (column >> 6) + 16 * zh + ((column >> 2) & 15)
    quarter = 32 - 32 * (((column >> 1) & 1) - (row & 1))
    values = sine((((row >> 1) & 31) - 16) * cell + quarter)
    return jnp.where((row >> 6) == (column & 1), values, 0.0)


def x_back_table(zh):
    row, column = grid_of(256, 128)
    cell = 32 * (row >> 6) + 16 * zh + ((row >> 2) & 15)
    quarter = 32 + 32 * ((column & 1) - ((row >> 1) & 1))
    values = sine((((column >> 1) & 31) - 16) * cell + quarter)
    return jnp.where((row & 1) == (column >> 6), values, 0.0)


def y_table(pencil_of):
    row, column = grid_of(128, 256)
    cell = 16 * pencil_of((column >> 3) & 15) + 2 * (column & 7) + (row >> 6)
    quarter = 32 - 32 * ((column >> 7) - ((row >> 5) & 1))
    return sine(((row & 31) - 16) * cell + quarter) * UNIT


def y_back_table():
    row, column = grid_of(128, 128)
    cell = 2 * (row & 63) + (column >> 6)
    quarter = 32 + 32 * (((column >> 5) & 1) - (row >> 6))
    return sine(((column & 31) - 16) * cell + quarter)


def pattern(keep):
    return jnp.where(keep, 1.0, 0.0).astype(BF16)


def make_grad(pre, out_grad, grad):
    def some(i, carry):
        rows = pl.ds(pl.multiple_of(i * 64, 64), 64)
        v = pre[rows, :]
        cdf = 0.5 * (1.0 + lax.erf(v * (1.0 / math.sqrt(2.0))))
        bump = v * jnp.exp(-0.5 * v * v) * (1.0 / math.sqrt(2.0 * math.pi))
        grad[rows, :] = out_grad[rows, :] * (cdf + bump)
        return carry

    lax.fori_loop(0, grad.shape[0] // 64, some, 0)


def front_kernel(layer, pre, out_grad, message, table, grad2):
    @pl.when(pl.program_id(0) + pl.program_id(1) == 0)
    def _():
        table[...] = jnp.concatenate(halves(z_table(1.0)), 0)

    layer, pre, out_grad = (ref.reshape(1024, 128) for ref in (layer, pre, out_grad))
    make_grad(pre, out_grad, grad2)
    for field, values in ((0, layer), (1, grad2)):
        for j in range(0, 4, 2):
            cells = [
                jnp.concatenate(
                    [values[pl.ds(x * 8 + 2 * j + y, 64, stride=16), :] for y in range(4)], 0
                )
                for x in range(2)
            ]
            top, rest = halves(jnp.concatenate(cells, 1))
            spectrum = dot(top, table[...], 1, 1)
            spectrum = spectrum[:, :128] + spectrum[:, 128:] + dot(rest, table[:128], 1, 1)
            spectrum = spectrum.T
            for k in range(2):
                part = spectrum[:, 128 * k : 128 * k + 128].reshape(16, 8, 128)
                message[:, field, 0, 8 * (j + k) : 8 * (j + k) + 8, :] = part


def local_kernel(point, layer, pre, out_grad, base, sums, products, grad):
    layer, pre, out_grad, base = (ref.reshape(1024, 128) for ref in (layer, pre, out_grad, base))
    make_grad(pre, out_grad, grad)
    step = pl.program_id(0) * 2 + pl.program_id(1)

    @pl.when(step == 0)
    def _():
        products[...] = jnp.zeros_like(products)

    for cell in range(0, 16, 2):
        u = jnp.concatenate([layer[pl.ds(cell + k, 64, stride=16), :] for k in range(2)], 1)
        g = jnp.concatenate([grad[pl.ds(cell + k, 64, stride=16), :] for k in range(2)], 1)
        products[...] += mm(u, g, 1, 1)
        mixed = mm(point[...], g)
        for k in range(2):
            base[pl.ds(cell + k, 64, stride=16), :] = mixed[:, 128 * k : 128 * k + 128]

    @pl.when(step == 3)
    def _():
        by_pair = products[0:32, 0:32] + products[32:64, 32:64]
        for k in range(4):
            sums[:, 32 * k : 32 * k + 32] = by_pair[8 * k : 8 * k + 8, :]


def weight_kernel(spread, codes, scales, noise, weight):
    step = jnp.exp2(scales[...].astype(F32) * -0.25) * (1.0 / (16.0 * math.sqrt(32.0)))
    top, rest = halves(step)
    last = (step - top.astype(F32) - rest.astype(F32)).astype(BF16)
    wide = sum(dot(part, spread[...]) for part in (last, rest, top))
    weight[...] = codes[...].astype(F32) * wide * (1.0 + noise[...])


def along_x(table, arrived, j):
    cells = [arrived[:, 0, :, 8 * k : 8 * k + 8, :].reshape(256, 128) for k in (j, j + 1)]
    return mm(table, jnp.concatenate(cells, 1))


def x_kernel(place, arrived, message):
    table = x_table(place[0])
    for j in range(0, 8, 2):
        modes = along_x(table, arrived, j)
        for k in range(2):
            message[:, j + k] = modes[:, 128 * k : 128 * k + 128].reshape(16, 8, 128)


def x_side_kernel(place, arrived, keep, give, tiles):
    table = x_table(place[0])
    for j in range(0, 8, 2):
        modes = along_x(table, arrived, j)
        for k in range(2):
            tiles[:, j + k] = modes[:, 128 * k : 128 * k + 128].reshape(16, 8, 128)
    for step in range(8):
        peer = 2 * ((place[3] + step) & 7)
        keep[step] = tiles[peer + place[4]]
        give[step] = tiles[peer + 1 - place[4]]


def pair_kernel(keep, got, *pairs):
    for step, pair in enumerate(pairs):
        pair[0] = keep[step]
        pair[1] = got[step]


def along_y(table, pieces):
    cells = [
        jnp.concatenate(
            [rows[pl.ds(at + 2 * kx + r, 8, stride=8), :] for r in range(2) for rows, at in pieces], 0
        )
        for kx in range(4)
    ]
    modes = mm(table, jnp.concatenate(cells, 1))
    modes = [modes[:, 128 * kx : 128 * kx + 128] for kx in range(4)]
    modes = [part[:64] + pltpu.roll(part[64:], 64, 1) for part in modes]
    real, imag = ([part[32 * r : 32 * r + 32] for part in modes] for r in range(2))
    return jnp.concatenate(real, 0), jnp.concatenate(imag, 0)


def mode_kernel(place, weight, arrived, g_there, message, g_hat, sent):
    sources = arrived.reshape(1024, 128)
    table = y_table(lambda source: source & 7)
    g_real, g_imag = along_y(table, [(sources, 64 * peer) for peer in range(16)])
    g_hat[0] = g_real
    g_hat[1] = g_imag
    store = pltpu.make_async_copy(g_hat, g_there, sent)
    store.start()
    row, column = grid_of(128, 128)
    row_long, column_long = grid_of(1024, 128)
    gather = pattern((row_long >> 5) == column_long)
    q_real = q_imag = None
    for b in range(2):
        wide = pattern(row == (column & 31) + 32 * b)
        wide_real, wide_imag = mm_exact(g_real, wide), mm_exact(g_imag, wide)
        real = imag = 0.0
        for part in range(4):
            lanes = slice(256 * part, 256 * part + 256)
            w_real = weight[:, 256 * part : 256 * part + 256]
            w_imag = weight[:, 1024 + 256 * part : 1280 + 256 * part]
            gr = jnp.concatenate([wide_real, wide_real], 1)
            gi = jnp.concatenate([wide_imag, wide_imag], 1)
            real += mm_exact(w_real * gr + w_imag * gi, gather[lanes])
            imag += mm_exact(w_real * gi - w_imag * gr, gather[lanes])
        if b == 0:
            q_real, q_imag = real, imag
        else:
            q_real, q_imag = q_real + pltpu.roll(real, 32, 1), q_imag + pltpu.roll(imag, 32, 1)
    rows = message.reshape(1024, 128)
    modes = [
        jnp.concatenate([q_real[32 * kx : 32 * kx + 32], q_imag[32 * kx : 32 * kx + 32]], 0)
        for kx in range(4)
    ]
    modes = [jnp.concatenate([part, pltpu.roll(part, 64, 1)], 0) for part in modes]
    cells = mm(y_back_table(), jnp.concatenate(modes, 1))
    for kx in range(4):
        for r in range(2):
            for zh in range(2):
                part = cells[64 * r : 64 * r + 64, 128 * kx : 128 * kx + 128]
                rows[pl.ds(512 * zh + 2 * kx + r, 64, stride=8), :] = part

    @pl.when(place[2] == 1)
    def _():
        bias = g_real[16:17] + pltpu.roll(g_real[16:17], 96, 1)
        rows[pl.ds(1, 16, stride=64), :] = jnp.broadcast_to(bias * (1.0 / (UNIT * CELLS)), (16, 128))

    store.wait()


def outer_kernel(place, *refs):
    *pairs, g_hat, result = refs

    def pencil(source):
        return 2 * ((place[3] - (source >> 1)) & 3) + ((source & 1) ^ place[4])

    pieces = [(pair.reshape(128, 128), 64 * k) for pair in pairs for k in range(2)]
    u_real, u_imag = along_y(y_table(pencil), pieces)
    row, column = grid_of(128, 128)
    u, g = [], []
    for b in range(2):
        wide = pattern(row == (column & 31) + 32 * b)
        u.append([pltpu.roll(v, 96, 1) if b else v for v in (u_real, u_imag)])
        g.append([mm_exact(g_hat[r], wide) for r in range(2)])
    g = [[jnp.concatenate([v, v], 1) for v in pair] for pair in g]
    row, column = grid_of(128, 256)
    for part in range(4):
        wide = pattern(row == (column >> 5) + 8 * part)
        real = imag = 0.0
        for b in range(2):
            ur, ui = (mm_exact(v, wide) for v in u[b])
            gr, gi = g[b]
            real += ur * gr + ui * gi
            imag += ur * gi - ui * gr
        result[:, 256 * part : 256 * part + 256] = real
        result[:, 1024 + 256 * part : 1280 + 256 * part] = imag


def x_back_kernel(place, arrived, sums, message):
    message[:, 16] = jnp.broadcast_to(sums[...][None], (16, 8, 128))
    table = x_back_table(place[0])
    for j in range(0, 8, 2):
        cells = jnp.concatenate([arrived[:, k].reshape(128, 128) for k in (j, j + 1)], 1)
        cells = mm(table, cells)
        for k in range(2):
            part = cells[:, 128 * k : 128 * k + 128].reshape(16, 2, 8, 128)
            message[:, j + k] = part[:, 0]
            message[:, 8 + j + k] = part[:, 1]

    @pl.when(place[1] == 1)
    def _():
        message[:, 0, 2:3] = jnp.broadcast_to(arrived[4, 0, 1:2][None], (16, 1, 128))


def end_kernel(arrived, sums, base, result, grad_point, grad_bias, table, held, taken):
    result = result.reshape(1024, 128)
    step = 2 * pl.program_id(0) + pl.program_id(1)

    def load(n):
        there = base.at[:, pl.ds(2 * (n // 2), 2), pl.ds(8 * (n % 2), 8), :]
        return pltpu.make_async_copy(there, held.at[n], taken.at[n])

    @pl.when(step == 0)
    def _():
        for n in range(4):
            load(n).start()
        table[...] = z_table(UNIT)
        total = jnp.sum(sums[:, 0], axis=0) * (1.0 / CELLS)
        for k in range(4):
            grad_point[8 * k : 8 * k + 8, :] = total[:, 32 * k : 32 * k + 32]
        grad_bias[...] = arrived[0, 0, 2:3, 0:32]

    for n in range(4):

        @pl.when(step == n)
        def _():
            load(n).wait()
            rest = held.at[n].reshape(1024, 128)
            for j in range(4):
                cells = mm(arrived[:, j].reshape(128, 128), table[...], 0, 0)
                for x in range(2):
                    for odd in range(2):
                        rows = pl.ds(x * 8 + 2 * j + odd, 64, stride=16)
                        part = cells[64 * odd : 64 * odd + 64, 128 * x : 128 * x + 128]
                        result[rows, :] = rest[rows, :] + part


def params(steps=0, mebibytes=20):
    return pltpu.CompilerParams(
        dimension_semantics=("arbitrary",) * steps if steps else None,
        vmem_limit_bytes=mebibytes << 20,
    )


def cost(flops, moved):
    return pl.CostEstimate(flops=flops, bytes_accessed=moved, transcendentals=0)


def whole(*shape):
    return pl.BlockSpec(shape, lambda *_: (0,) * len(shape))


def shaped(*shape):
    return jax.ShapeDtypeStruct(shape, F32)


def exchange(message, axes):
    return lax.all_to_all(message, axes, split_axis=0, concat_axis=0, tiled=True)


def per_device(
    layer_input, pre_act, out_grad, weight_codes, scale_codes, weight_noise, point_weight
):
    layer, pre, slope_in = (v.reshape(64, 4, 16, 128) for v in (layer_input, pre_act, out_grad))
    plane_first = (lax.axis_index("yp") + lax.axis_index("xp") == 0).astype(jnp.int32)
    owner = plane_first * (lax.axis_index(COLUMN) == 4).astype(jnp.int32)
    chip, core = lax.axis_index(("zh", "zl")), lax.axis_index("co")
    place = jnp.stack([lax.axis_index("zh"), plane_first, owner, chip, core]).astype(jnp.int32)
    mega = 1 << 20
    field = pl.BlockSpec((64, 2, 8, 128), lambda p, h: (0, p, h, 0))
    message = pl.pallas_call(
        front_kernel,
        grid=(2, 2),
        in_specs=[field, field, field],
        out_specs=pl.BlockSpec((16, 2, 1, 32, 128), lambda p, h: (0, 0, p, h, 0)),
        out_shape=shaped(16, 2, 2, 64, 128),
        scratch_shapes=[pltpu.VMEM((256, 256), BF16), pltpu.VMEM((1024, 128), F32)],
        compiler_params=params(2, 60),
        cost_estimate=cost(1 << 30, 10 * mega),
        name="front",
    )(layer, pre, slope_in)
    arrived = exchange(message, PLANE)

    blocks = np.kron(np.eye(2, dtype=np.float32), np.ones((32, 32), np.float32))
    both = jnp.tile(point_weight, (2, 2)) * blocks
    base, sums = pl.pallas_call(
        local_kernel,
        grid=(2, 2),
        in_specs=[whole(64, 64), field, field, field],
        out_specs=[field, whole(8, 128)],
        out_shape=[shaped(64, 4, 16, 128), shaped(8, 128)],
        scratch_shapes=[pltpu.VMEM((64, 64), F32), pltpu.VMEM((1024, 128), F32)],
        compiler_params=params(2, 60),
        cost_estimate=cost(1 << 30, 8 * mega),
        name="local",
    )(both, layer, pre, slope_in)

    for axes, size, bit in (("co", 2, 1), ("zl", 4, 1), ("zl", 4, 2), ("zh", 2, 1)):
        sums = sums + lax.ppermute(sums, axes, [(i, i ^ bit) for i in range(size)])
    arrived, sums = lax.optimization_barrier((arrived, sums))

    spread = np.kron(np.eye(64, dtype=np.float32), np.ones((1, 32), np.float32))
    column = pl.BlockSpec((128, 512), lambda i: (0, i))
    codes, _ = lax.optimization_barrier((weight_codes, sums))
    weight = pl.pallas_call(
        weight_kernel,
        grid=(4,),
        in_specs=[pl.BlockSpec((64, 512), lambda i: (0, i)), column, whole(128, 64), column],
        out_specs=column,
        out_shape=shaped(128, 2048),
        compiler_params=params(1),
        cost_estimate=cost(1 << 27, 3 * mega),
        name="weight",
    )(
        jnp.asarray(spread, BF16),
        codes.reshape(128, 2048),
        scale_codes.reshape(128, 64),
        weight_noise.reshape(128, 2048),
    )

    def placed(in_specs, out_specs, scratch=()):
        return pltpu.PrefetchScalarGridSpec(
            num_scalar_prefetch=1,
            grid=(1,),
            in_specs=in_specs,
            out_specs=out_specs,
            scratch_shapes=scratch,
        )

    in_hbm = pl.BlockSpec(memory_space=pltpu.HBM)

    def one_field(index):
        return pl.BlockSpec((16, 1, 2, 64, 128), lambda *_: (0, index, 0, 0, 0))

    message = pl.pallas_call(
        x_kernel,
        grid_spec=placed([one_field(1)], whole(16, 8, 8, 128)),
        out_shape=shaped(16, 8, 8, 128),
        compiler_params=params(1),
        cost_estimate=cost(1 << 29, 2 * mega),
        name="x_modes",
    )(place, arrived)
    keep, give = pl.pallas_call(
        x_side_kernel,
        grid_spec=placed(
            [one_field(0)], [whole(8, 8, 8, 128)] * 2, [pltpu.VMEM((16, 8, 8, 128), F32)]
        ),
        out_shape=[shaped(8, 8, 8, 128)] * 2,
        compiler_params=params(1),
        cost_estimate=cost(1 << 29, 2 * mega),
        name="x_side",
    )(place, arrived)
    arrived = exchange(message, COLUMN)
    got = lax.ppermute(give, "co", [(0, 1), (1, 0)])
    pairs = pl.pallas_call(
        pair_kernel,
        grid=(1,),
        in_specs=[whole(8, 8, 8, 128)] * 2,
        out_specs=[whole(2, 8, 8, 128)] * 8,
        out_shape=[pltpu.HBM((2, 8, 8, 128), F32)] * 8,
        compiler_params=params(1),
        cost_estimate=cost(1 << 20, mega),
        name="pair",
    )(keep, got)

    def hop(step):
        route = [(chip, (chip + step) % 8) for chip in range(8)]
        return lax.ppermute(pairs[step], ("zh", "zl"), route)

    sent = {0: pairs[0]}
    weight, sent, pairs = lax.optimization_barrier((weight, sent, pairs))
    g_hat, message = pl.pallas_call(
        mode_kernel,
        grid_spec=placed(
            [whole(128, 2048), whole(16, 8, 8, 128)],
            [in_hbm, whole(16, 8, 8, 128)],
            [pltpu.VMEM((2, 128, 128), F32), pltpu.SemaphoreType.DMA],
        ),
        out_shape=[pltpu.HBM((2, 128, 128), F32), shaped(16, 8, 8, 128)],
        compiler_params=params(1),
        cost_estimate=cost(1 << 30, 3 * mega),
        name="modes",
    )(place, weight, arrived)
    returned = exchange(message, COLUMN)
    sent.update((step, hop(step)) for step in (1,7,2,6))
    returned, sent = lax.optimization_barrier((returned, sent))

    message = pl.pallas_call(
        x_back_kernel,
        grid_spec=placed([whole(16, 8, 8, 128), whole(8, 128)], whole(16, 17, 8, 128)),
        out_shape=shaped(16, 17, 8, 128),
        compiler_params=params(1),
        cost_estimate=cost(1 << 29, 2 * mega),
        name="x_cells",
    )(place, returned, sums)
    returned = exchange(message, PLANE)

    pairs, _ = lax.optimization_barrier((pairs, message))
    sent.update((step, hop(step)) for step in range(1, 8) if step not in sent)
    grad_spectral = pl.pallas_call(
        outer_kernel,
        grid_spec=placed([whole(2, 8, 8, 128)] * 8 + [whole(2, 128, 128)], whole(128, 2048)),
        out_shape=shaped(128, 2048),
        compiler_params=params(1, 60),
        cost_estimate=cost(1 << 30, 4 * mega),
        name="outer",
    )(place, *(sent[step] for step in range(8)), g_hat)

    grad_input, grad_point, grad_bias = pl.pallas_call(
        end_kernel,
        grid=(2, 2),
        in_specs=[
            pl.BlockSpec((16, 4, 8, 128), lambda p, h: (0, 2 * p + h, 0, 0)),
            pl.BlockSpec((16, 1, 8, 128), lambda p, h: (0, 16, 0, 0)),
            in_hbm,
        ],
        out_specs=[field, whole(32, 32), whole(1, 32)],
        out_shape=[shaped(64, 4, 16, 128), shaped(32, 32), shaped(1, 32)],
        scratch_shapes=[
            pltpu.VMEM((128, 256), F32),
            pltpu.VMEM((4, 64, 2, 8, 128), F32),
            pltpu.SemaphoreType.DMA((4,)),
        ],
        compiler_params=params(2),
        cost_estimate=cost(1 << 29, 5 * mega),
        name="end",
    )(returned, returned, base)
    return (
        grad_input.reshape(layer_input.shape),
        grad_spectral.reshape(weight_codes.shape),
        grad_point,
        grad_bias.reshape(32),
    )


def solution(mesh):
    fine = Mesh(mesh.devices.reshape(4, 2, 4, 4, 2), ("yp", "zh", "xp", "zl", "co"))
    slab, pencil = ("yp", "zh", "xp"), ("zl", "co")
    field, modes = P(None, None, slab, pencil, None), P(slab, pencil, None, None)
    return jax.shard_map(
        per_device,
        mesh=fine,
        in_specs=(field, field, field, modes, modes, modes, P()),
        out_specs=(field, modes, P(), P()),
        check_vma=False,
    )
```
